32 devices in a mesh: shard: 8 (over z, x), grp: 4 (over y, core).
Axes of the slice: x: 2, y: 2, z: 4, core: 2. Of those that a mesh axis runs over, the one named last changes fastest.
Arguments:
- embeddings: bfloat16 [8192, 1024], P('shard', 'grp')
- clusters: int32 [8192], P('shard'), may hold values from 0 to 3, as said below
- blocks: int32 [32, 4], P('shard'), may hold values from 0 to 31, as said below
- counts: int32 [32], P('shard'), may hold values from 1 to 4
- seed_mask: int32 [8192], P(('shard', 'grp')), may hold values 0 or 1
- prior: bfloat16 [8192, 256], P(('shard', 'grp')), may hold values from 0 to 1
Outputs:
- labels: bfloat16 [8192, 256], P(('shard', 'grp'))
The draws below stay inside these ranges and needn't reach their ends.
Inputs may be any that keep to these rules, and one draw needn't show every extreme that they name: `blocks`: slot 0 of row tile r is r itself; the other slots hold distinct tiles of the same shard or of the first 2 tiles of the next shard, never past the last tile; slots at or past counts hold such tiles too but carry no affinity. `clusters`: images 2m and 2m + 1 share a cluster.
All inputs are finite; a program needn't handle non-finite values. No bound on the sum of `seed_mask` on one device may be relied on, other than what follows from the above.
Results may differ from the reference program's by a relative error of at most 0.0038.
Values may be sent and summed in bfloat16 or wider, within the bound.
No kernel may reach another device: no remote copies, remote signals or barrier semaphores. Data moves between devices by JAX's collectives and lax.ppermute only.
A program may use at most 64 MiB of HBM per device.

```python
import jax
import jax.numpy as jnp
from jax import lax

D = 1024
C = 256
TILE = 256
K = 4
CLUSTERS = 4
STEPS = 2
TPS = 4
ROW_TILES = 32
IMAGES = 8192
WINDOW = 6


def draw_embeddings(key, part):
    first = jax.random.fold_in(key, 0)
    values = jnp.clip(jax.random.normal(first, (IMAGES, D), jnp.float32), -6.0, 6.0)
    return (values / jnp.sqrt(jnp.float32(D))).astype(jnp.bfloat16)


def draw_clusters(key, part):
    paired = jax.random.randint(key, (IMAGES // 2,), 0, CLUSTERS)
    return jnp.repeat(paired, 2).astype(jnp.int32)


def draw_blocks(key, part):
    rows = jnp.arange(ROW_TILES, dtype=jnp.int32)
    base = rows // TPS * TPS
    offsets = jnp.arange(WINDOW, dtype=jnp.int32)
    candidates = base[:, None] + offsets[None, :]
    usable = (candidates < ROW_TILES) & (candidates != rows[:, None])
    scores = jax.random.randint(key, (ROW_TILES, WINDOW), 0, 1 << 20) * WINDOW + offsets[None, :]
    scores = jnp.where(usable, scores, 1 << 30)
    order = jnp.argsort(scores, axis=1, stable=True)
    picked = jnp.take_along_axis(candidates, order[:, :K - 1], axis=1)
    return jnp.concatenate([rows[:, None], picked], axis=1).astype(jnp.int32)


def place_ends(entries, key, low, high):
    place = [jax.random.randint(jax.random.fold_in(key, axis), (), 0, length) for axis, length in enumerate(entries.shape)]
    widest = entries.shape.index(max(entries.shape))
    neighbour = place[:widest] + [(place[widest] + 1) % entries.shape[widest]] + place[widest + 1:]
    return entries.at[tuple(place)].set(low).at[tuple(neighbour)].set(high)


def levels(rng, extent, cuts, smallest, largest):
    def one(dim, parts):
        heights = jax.random.uniform(jax.random.fold_in(jax.random.fold_in(rng, 6), dim), (parts,), jnp.float32, smallest / len(cuts), largest / len(cuts))
        return jnp.repeat(jnp.exp(heights), extent[dim] // parts).reshape((-1,) + (1,) * (len(extent) - dim - 1))

    gain = one(*cuts[0])
    for cut in cuts[1:]:
        gain = gain * one(*cut)
    return gain


def setup_inputs(seed: int = 0) -> dict:
    arg_keys = jax.random.split(jax.random.key(seed), 7)
    return {
        "embeddings": draw_embeddings(jax.random.fold_in(arg_keys[6], 71), 0),
        "clusters": draw_clusters(jax.random.fold_in(arg_keys[6], 71), 0),
        "blocks": draw_blocks(jax.random.fold_in(arg_keys[6], 71), 0),
        "counts": place_ends(jax.random.randint(arg_keys[3], (ROW_TILES,), 1, K + 1), jax.random.fold_in(arg_keys[3], 1), 1, K).astype(jnp.int32),
        "seed_mask": place_ends((jax.random.randint(arg_keys[4], (IMAGES,), 0, 4) < 1).astype(jnp.int32), jax.random.fold_in(arg_keys[4], 1), 0, 1),
        "prior": jnp.clip(1.0 * jax.random.uniform(arg_keys[5], (IMAGES, C), jnp.float32) ** levels(arg_keys[5], (IMAGES, C), ((0, 32),), -0.2, 0.2), 0.0, 1.0).astype(jnp.bfloat16),
    }


kernel_width = 0.06
spread_weight = 0.6


def reference(embeddings, clusters, blocks, counts, seed_mask, prior):
    tiles_x = embeddings.reshape(ROW_TILES, TILE, D)
    norms = jnp.sum(jnp.square(embeddings.astype(jnp.float32)), axis=-1).reshape(ROW_TILES, TILE)
    tiles_c = clusters.reshape(ROW_TILES, TILE)
    slot_index = jnp.arange(K, dtype=jnp.int32)
    image_index = jnp.arange(TILE, dtype=jnp.int32)

    def affinity_of(row):
        ids = blocks[row]
        rows_x = tiles_x[row].astype(jnp.float32)
        cols_x = tiles_x[ids].astype(jnp.float32)
        dots = jnp.einsum("if,kjf->ikj", rows_x, cols_x, precision=lax.Precision.HIGHEST)
        dist = norms[row][:, None, None] + norms[ids][None, :, :] - 2.0 * dots
        live = slot_index < counts[row]
        same = tiles_c[row][:, None, None] == tiles_c[ids][None, :, :]
        itself = (ids[None, :, None] == row) & (image_index[:, None, None] == image_index[None, None, :])
        allowed = same & live[None, :, None] & jnp.logical_not(itself)
        logits = -dist / kernel_width
        top = jnp.max(jnp.where(allowed, logits, jnp.float32(-1e30)), axis=(1, 2), keepdims=True)
        weights = jnp.where(allowed, jnp.exp(logits - top), jnp.float32(0.0))
        total = jnp.sum(weights, axis=(1, 2), keepdims=True)
        return (weights / total).astype(jnp.bfloat16)

    all_rows = jnp.arange(ROW_TILES, dtype=jnp.int32)
    affinity = lax.map(affinity_of, all_rows)
    seeds = (seed_mask.astype(jnp.float32)[:, None] * prior.astype(jnp.float32)).reshape(ROW_TILES, TILE, C)
    labels = seeds.astype(jnp.bfloat16)
    for step in range(STEPS):
        current = labels

        def spread_of(row):
            picked = current[blocks[row]].astype(jnp.float32)
            spread = jnp.einsum("ikj,kjc->ic", affinity[row].astype(jnp.float32), picked, precision=lax.Precision.HIGHEST)
            return (spread_weight * spread + (1.0 - spread_weight) * seeds[row]).astype(jnp.bfloat16)

        labels = lax.map(spread_of, all_rows)
    return labels.reshape(IMAGES, C)
```

```python
import functools

import jax
import jax.numpy as jnp
from jax import lax
from jax.experimental import pallas as pl
from jax.experimental.pallas import tpu as pltpu
from jax.sharding import PartitionSpec as P

TILE = 256
K = 4
SPILL = 2
ROWS = 32

kernel_width = 0.06
spread_weight = 0.6
MASKED = -1e30

NT = (((1,), (1,)), ((), ()))


def across(block, distance):
    groups = lax.axis_size("grp")
    return lax.ppermute(block, "grp", [(i, i ^ distance) for i in range(groups)])


def from_next(block):
    return lax.ppermute(block, "shard", [(i + 1, i) for i in range(lax.axis_size("shard") - 1)])


def from_next_heads(block, pair):
    groups = lax.axis_size("grp")
    route = [
        ((i + 1) * groups + c, i * groups + 2 * pair + c)
        for i in range(lax.axis_size("shard") - 1)
        for c in range(2)
    ]
    return lax.ppermute(block, ("shard", "grp"), route)


def listed(blocks_ref, counts_ref, groups):
    member = lax.axis_index("grp")
    base = lax.axis_index("shard") * groups
    count = counts_ref[member]
    ids = [blocks_ref[member, k] - base for k in range(K)]
    return [
        sum(jnp.where((ids[k] == w) & (k < count), 1, 0) for k in range(K))
        for w in range(groups + SPILL)
    ]


def spread(aff_ref, own_refs, spill_refs, seed, groups):
    member = lax.axis_index("grp")
    core = lax.rem(member, 2)
    total = jnp.zeros(seed.shape, jnp.float32)
    for m, ref in enumerate(own_refs):
        total += jnp.dot(aff_ref[member ^ m], ref[...], preferred_element_type=jnp.float32)
    for m, ref in enumerate(spill_refs):
        total += jnp.dot(
            aff_ref[groups + (core ^ m)], ref[...], preferred_element_type=jnp.float32
        )
    return (spread_weight * total + (1.0 - spread_weight) * seed.astype(jnp.float32)).astype(
        jnp.bfloat16
    )


def affinity_kernel(groups, blocks_ref, counts_ref, clusters_ref, spill_c_ref, *refs):
    quarters = groups
    half = groups // 2
    wtiles = groups + SPILL
    refs = list(refs)
    own_x = [[refs.pop(0) for _ in range(1 if q < 2 else 2)] for q in range(quarters)]
    spill_x = [refs.pop(0) for _ in range(quarters)]
    own_l = [refs.pop(0) for _ in range(groups)]
    spill_l = [refs.pop(0) for _ in range(SPILL)]
    labels_ref, aff_ref, rows_ref, logit_ref, normi_ref = refs
    member = lax.axis_index("grp")
    mult = listed(blocks_ref, counts_ref, groups)
    spill_rows = SPILL * TILE

    for q in range(quarters):
        if len(own_x[q]) == 1:
            rows_ref[q] = own_x[q][0][pl.ds(pl.multiple_of(member * TILE, TILE), TILE), :]
        else:
            @pl.when(member < SPILL)
            def _(q=q):
                rows_ref[q] = own_x[q][0][pl.ds(pl.multiple_of(member * TILE, TILE), TILE), :]

            @pl.when(member >= SPILL)
            def _(q=q):
                at = pl.multiple_of((member - SPILL) * TILE, TILE)
                rows_ref[q] = own_x[q][1][pl.ds(at, TILE), :]

    def columns(w, q):
        if w >= groups:
            return spill_x[q][(w - groups) * TILE:(w - groups + 1) * TILE, :]
        if len(own_x[q]) == 1:
            return own_x[q][0][w * TILE:(w + 1) * TILE, :]
        if w < SPILL:
            return own_x[q][0][w * TILE:(w + 1) * TILE, :]
        return own_x[q][1][(w - SPILL) * TILE:(w - SPILL + 1) * TILE, :]

    def cluster_row(w):
        if w >= groups:
            return spill_c_ref[:, (w - groups) * TILE:(w - groups + 1) * TILE]
        return clusters_ref[:, w * TILE:(w + 1) * TILE]

    eye = lax.broadcasted_iota(jnp.int32, (TILE, TILE), 0) == lax.broadcasted_iota(
        jnp.int32, (TILE, TILE), 1
    )

    def as_column(row):
        return jnp.sum(jnp.where(eye, row, jnp.zeros_like(row)), axis=1, keepdims=True)

    def norm_row(tiles):
        squares = sum(
            jnp.square(t[:, h * 128:(h + 1) * 128].astype(jnp.float32))
            for t in tiles
            for h in range(t.shape[1] // 128)
        )
        ones = jnp.ones((8, 128), jnp.float32)
        return lax.dot_general(
            ones, squares, NT, precision=lax.Precision.HIGHEST,
            preferred_element_type=jnp.float32,
        )[0:1]

    own_n = norm_row([rows_ref[q] for q in range(quarters)])
    normi = as_column(own_n)
    own_c = clusters_ref[:, pl.ds(pl.multiple_of(member * TILE, TILE), TILE)]
    row_c = as_column(own_c.astype(jnp.float32))

    for w in range(wtiles):
        @pl.when(mult[w] > 0)
        def _(w=w):
            tiles = [columns(w, q) for q in range(quarters)]
            norm = norm_row(tiles)
            dots = sum(
                lax.dot_general(rows_ref[q], tiles[q], NT, preferred_element_type=jnp.float32)
                for q in range(quarters)
            )
            dist = normi + norm - 2.0 * dots
            same = row_c == cluster_row(w).astype(jnp.float32)
            allowed = same & jnp.logical_not(eye & (member == w))
            logit_ref[w] = jnp.where(allowed, dist * (-1.0 / kernel_width), MASKED)

        @pl.when(mult[w] == 0)
        def _(w=w):
            logit_ref[w] = jnp.full((TILE, TILE), MASKED, jnp.float32)

    factors = [m.astype(jnp.float32) for m in mult]

    def softmax(step, carry):
        rows = pl.ds(pl.multiple_of(step * ROWS, ROWS), ROWS)
        logits = [logit_ref[w, rows, :] for w in range(wtiles)]
        top = functools.reduce(jnp.maximum, logits)
        top = jnp.max(top, axis=1, keepdims=True)
        weights = [jnp.exp(logits[w] - top) * factors[w] for w in range(wtiles)]
        total = jnp.sum(functools.reduce(jnp.add, weights), axis=1, keepdims=True)
        scale = 1.0 / total
        for w in range(wtiles):
            aff_ref[w, rows, :] = (weights[w] * scale).astype(jnp.bfloat16)
        return carry

    lax.fori_loop(0, TILE // ROWS, softmax, 0, unroll=True)
    labels_ref[...] = spread(aff_ref, own_l, spill_l, own_l[0][...], groups)


def spread_kernel(groups, aff_ref, seed_ref, *refs):
    own_l = refs[:groups]
    spill_parts = refs[groups:-2]
    out_ref, got_ref = refs[-2:]
    pair = lax.axis_index("grp") // 2
    for k in range(groups // 2):
        @pl.when(pair == k)
        def _(k=k):
            for t in range(SPILL):
                got_ref[t] = spill_parts[k * SPILL + t][...]
    out_ref[...] = spread(
        aff_ref, own_l, [got_ref.at[t] for t in range(SPILL)], seed_ref[...], groups
    )


def local(embeddings, clusters, blocks, counts, seed_mask, prior):
    groups = lax.axis_size("grp")
    member = lax.axis_index("grp")
    spill_rows = SPILL * TILE
    width = prior.shape[1]

    head, tail = embeddings[:spill_rows], embeddings[spill_rows:]
    seeds = seed_mask.astype(jnp.bfloat16)[:, None] * prior

    own_x, spill_x = [], []
    head_far = [across(head, 2 * m) for m in range(1, groups // 2)]
    spill_near = from_next(head)
    spill_c = from_next(clusters[:spill_rows])
    tail_far = [across(tail, 2 * m) for m in range(1, groups // 2)]
    own_sib = across(embeddings, 1)
    spill_far = [from_next(h) for h in head_far]
    labels_far = [across(seeds, 2 * m) for m in range(1, groups // 2)]
    first = seeds
    for m in range(1, groups // 2):
        first = jnp.where(member // 2 == m, labels_far[m - 1], first)
    spill_l0 = from_next(first)

    own_x = [[embeddings], [own_sib]]
    spill_x = [spill_near, across(spill_near, 1)]
    own_l = [seeds, across(seeds, 1)]
    for m in range(groups // 2 - 1):
        own_x += [[head_far[m], tail_far[m]], [across(head_far[m], 1), across(tail_far[m], 1)]]
        spill_x += [spill_far[m], across(spill_far[m], 1)]
        own_l += [labels_far[m], across(labels_far[m], 1)]
    spill_l = [spill_l0, across(spill_l0, 1)]

    arrays = [x for xs in own_x for x in xs] + spill_x + own_l + spill_l
    smem = pl.BlockSpec(memory_space=pltpu.SMEM)
    vmem = pl.BlockSpec(memory_space=pltpu.VMEM)
    wtiles = groups + SPILL
    labels, affinity = pl.pallas_call(
        functools.partial(affinity_kernel, groups),
        out_shape=(
            jax.ShapeDtypeStruct((TILE, width), jnp.bfloat16),
            jax.ShapeDtypeStruct((wtiles, TILE, TILE), jnp.bfloat16),
        ),
        in_specs=[smem, smem] + [vmem] * (2 + len(arrays)),
        out_specs=(vmem, vmem),
        scratch_shapes=[
            pltpu.VMEM((groups, TILE, embeddings.shape[1]), jnp.bfloat16),
            pltpu.VMEM((wtiles, TILE, TILE), jnp.float32),
            pltpu.VMEM((TILE, 1), jnp.float32),
        ],
        compiler_params=pltpu.CompilerParams(vmem_limit_bytes=40 * 1024 * 1024),
        name="affinity",
    )(blocks, counts, clusters.reshape(1, -1), spill_c.reshape(1, -1), *arrays)

    far = [across(labels, 2 * m) for m in range(1, groups // 2)]
    heads = [from_next_heads(labels, m) for m in range(groups // 2)]
    own_l = [labels, across(labels, 1)]
    for f in far:
        own_l += [f, across(f, 1)]
    parts = []
    for h in heads:
        parts += [h, across(h, 1)]
    return pl.pallas_call(
        functools.partial(spread_kernel, groups),
        out_shape=jax.ShapeDtypeStruct((TILE, width), jnp.bfloat16),
        in_specs=[vmem] * (2 + groups + len(parts)),
        out_specs=vmem,
        scratch_shapes=[pltpu.VMEM((SPILL, TILE, width), jnp.bfloat16)],
        compiler_params=pltpu.CompilerParams(vmem_limit_bytes=40 * 1024 * 1024),
        name="spread",
    )(affinity, seeds, *own_l, *parts)


def solution(mesh):
    in_specs = (
        P("shard", "grp"),
        P("shard"),
        P("shard", None),
        P("shard"),
        P(("shard", "grp")),
        P(("shard", "grp"), None),
    )
    out_specs = P(("shard", "grp"), None)
    return jax.shard_map(local, mesh=mesh, in_specs=in_specs, out_specs=out_specs, check_vma=False)
```

```python
import functools

import jax
import jax.numpy as jnp
from jax import lax
from jax.experimental import pallas as pl
from jax.experimental.pallas import tpu as pltpu
from jax.sharding import PartitionSpec as P

TILE = 256
K = 4
SPILL = 2
ROWS = 32

kernel_width = 0.06
spread_weight = 0.6
MASKED = -1e30
LOG2E = 1.4426950408889634

NT = (((1,), (1,)), ((), ()))


def across(block, distance):
    groups = lax.axis_size("grp")
    return lax.ppermute(block, "grp", [(i, i ^ distance) for i in range(groups)])


def from_next(block, distance=0):
    groups = lax.axis_size("grp")
    shards = lax.axis_size("shard")
    if distance == 0:
        return lax.ppermute(block, "shard", [(i + 1, i) for i in range(shards - 1)])
    route = [
        ((i + 1) * groups + (g ^ distance), i * groups + g)
        for i in range(shards - 1)
        for g in range(groups)
    ]
    return lax.ppermute(block, ("shard", "grp"), route)


def after(block, done):
    return lax.optimization_barrier((block, done))[0]


def listed(blocks_ref, counts_ref, tile, groups):
    base = lax.axis_index("shard") * groups
    count = counts_ref[tile]
    ids = [blocks_ref[tile, k] - base for k in range(K)]
    return [
        sum(jnp.where((ids[k] == w) & (k < count), 1, 0) for k in range(K))
        for w in range(groups + SPILL)
    ]


def code_kernel(
    groups, blocks_ref, counts_ref, clusters_ref, spill_ref, code_ref, factor_ref, row_ref
):
    core = lax.rem(lax.axis_index("grp"), 2)
    eye = lax.broadcasted_iota(jnp.int32, (TILE, TILE), 0) == lax.broadcasted_iota(
        jnp.int32, (TILE, TILE), 1
    )
    packed = spill_ref[SPILL * TILE:, :].astype(jnp.float32)
    width = packed.shape[1]
    spilled = [
        jnp.concatenate(
            [packed[i // width:i // width + 1, :] for i in range(t * TILE, (t + 1) * TILE, width)],
            axis=1,
        )
        for t in range(SPILL)
    ]
    for m in range(groups // 2):
        tile = 2 * m + core
        mult = listed(blocks_ref, counts_ref, tile, groups)
        for w in range(groups + SPILL):
            if w < groups:
                row = clusters_ref[:, w * TILE:(w + 1) * TILE].astype(jnp.float32)
            else:
                row = spilled[w - groups]
            factor = jnp.full((1, TILE), mult[w].astype(jnp.float32))
            here = (slice(m * 8, m * 8 + 8), slice(w * TILE, (w + 1) * TILE))
            code_ref[here] = jnp.broadcast_to(jnp.where(factor > 0, row, -1.0), (8, TILE))
            factor_ref[here] = jnp.broadcast_to(factor, (8, TILE))
        own = clusters_ref[:, pl.ds(pl.multiple_of(tile * TILE, TILE), TILE)].astype(jnp.float32)
        column = jnp.sum(jnp.where(eye, own, jnp.zeros_like(own)), axis=1, keepdims=True)
        row_ref[m * TILE:(m + 1) * TILE, :] = jnp.broadcast_to(column, (TILE, 128))


def spread(aff_ref, parts, seed):
    total = jnp.zeros(seed.shape, jnp.float32)
    for w, ref in parts:
        total += jnp.dot(aff_ref[w], ref[...], preferred_element_type=jnp.float32)
    return (spread_weight * total + (1.0 - spread_weight) * seed.astype(jnp.float32)).astype(
        jnp.bfloat16
    )


def affinity_kernel(groups, m, windows, code_ref, factor_ref, row_ref, *refs):
    quarters = groups
    half = groups // 2
    wtiles = groups + SPILL
    ins, (aff_ref, labels_ref, logit_ref) = refs[:-3], refs[-3:]
    member = lax.axis_index("grp")
    core = lax.rem(member, 2)
    pair = member // 2
    tile = 2 * m + core
    scale = LOG2E / kernel_width

    def piece(at):
        ref, row = at
        return ins[ref].at[row:row + TILE, :]

    def columns(w, q):
        return piece(windows["x"][q][w])[...]

    def squares(tiles):
        return functools.reduce(
            jnp.add,
            [
                jnp.square(t[:, h * 128:(h + 1) * 128].astype(jnp.float32))
                for t in tiles
                for h in range(t.shape[1] // 128)
            ],
        )

    rows = [
        jnp.where(core == 0, columns(2 * m, q), columns(2 * m + 1, q)) for q in range(quarters)
    ]
    row_n = jnp.sum(squares(rows), axis=1, keepdims=True) * scale
    row_c = row_ref[m * TILE:(m + 1) * TILE, 0:1]
    eye = lax.broadcasted_iota(jnp.int32, (TILE, TILE), 0) == lax.broadcasted_iota(
        jnp.int32, (TILE, TILE), 1
    )
    for w in range(wtiles):
        tiles = [columns(w, q) for q in range(quarters)]
        column_n = jnp.sum(squares(tiles).T, axis=0, keepdims=True) * scale
        dots = functools.reduce(
            jnp.add,
            [
                lax.dot_general(rows[q], tiles[q], NT, preferred_element_type=jnp.float32)
                for q in range(quarters)
            ],
        )
        allowed = row_c == code_ref[m * 8:m * 8 + 1, w * TILE:(w + 1) * TILE]
        if w // 2 == m:
            allowed = allowed & jnp.logical_not(eye & (tile == w))
        logit_ref[w] = jnp.where(allowed, dots * (2.0 * scale) - column_n - row_n, MASKED)

    def softmax(step, carry):
        at = pl.ds(pl.multiple_of(step * ROWS, ROWS), ROWS)
        logits = [logit_ref[w, at, :] for w in range(wtiles)]
        top = jnp.max(functools.reduce(jnp.maximum, logits), axis=1, keepdims=True)
        weights = [
            jnp.exp2(logits[w] - top) * factor_ref[m * 8:m * 8 + 1, w * TILE:(w + 1) * TILE]
            for w in range(wtiles)
        ]
        total = jnp.sum(functools.reduce(jnp.add, weights), axis=1, keepdims=True)
        share = 1.0 / total
        for w in range(wtiles):
            aff_ref[w, at, :] = (weights[w] * share).astype(jnp.bfloat16)
        return carry

    lax.fori_loop(0, TILE // ROWS, softmax, 0, unroll=True)

    parts = []
    for r in range(half):
        parts.append((2 * (pair ^ r) + core, piece(windows["mine"][r])))
        parts.append((2 * (pair ^ r) + 1 - core, piece(windows["other"][r])))
    parts.append((groups + core, piece(windows["mine"][half])))
    parts.append((groups + 1 - core, piece(windows["other"][half])))
    seed = piece(windows["mine"][0])[...]
    for r in range(1, half):
        seed = jnp.where((pair ^ m) == r, piece(windows["mine"][r])[...], seed)
    labels_ref[...] = spread(aff_ref, parts, seed)


def last_kernel(groups, seed_ref, *refs):
    half = groups // 2
    core = lax.rem(lax.axis_index("grp"), 2)
    affs, mine, other = refs[:half], refs[half:2 * half + 1], refs[2 * half + 1:3 * half + 2]
    parts = []
    for m in range(half + 1):
        parts += [(2 * m + core, mine[m]), (2 * m + 1 - core, other[m])]
    for m in range(half):
        @pl.when(lax.axis_index("grp") // 2 == m)
        def _(m=m):
            refs[-1][...] = spread(affs[m], parts, seed_ref[...])


def local(embeddings, clusters, blocks, counts, seed_mask, prior):
    groups = lax.axis_size("grp")
    half = groups // 2
    apart = range(1, half)
    pair = lax.axis_index("grp") // 2
    width = embeddings.shape[1]
    concepts = prior.shape[1]
    wtiles = groups + SPILL
    head_rows = SPILL * TILE

    seeds = jnp.where(seed_mask[:, None] > 0, prior, jnp.zeros_like(prior))
    first = embeddings[:TILE]
    rest = embeddings[TILE:]
    head_c = clusters[:head_rows].astype(jnp.bfloat16).reshape(-1, width)
    head_c = jnp.pad(head_c, ((0, 16 - head_c.shape[0]), (0, 0)))
    packed = width == concepts
    if packed:
        first_out = jnp.concatenate([first, seeds])
        first_far = [across(first_out, 2 * m) for m in apart]
        seeds_far = [f[TILE:] for f in first_far]
    else:
        first_far = [across(first, 2 * m) for m in apart]
        seeds_far = [across(seeds, 2 * m) for m in apart]
    rest_far = [across(rest, 2 * m) for m in apart]
    near = from_next(jnp.concatenate([embeddings[:head_rows], head_c]))
    head_seeds = seeds
    for m in apart:
        head_seeds = jnp.where(pair == m, seeds_far[m - 1], head_seeds)
    if packed:
        first_on = [jnp.concatenate([first_far[0][:TILE], head_seeds])]
        first_on += [f[:TILE] for f in first_far[1:]]
        near_first = [from_next(f) for f in first_on]
    else:
        near_first = [from_next(f) for f in first_far]
        near_seeds = from_next(head_seeds)
    second = embeddings[TILE:head_rows]
    near_second = [from_next(second, 2 * m) for m in apart]

    own_other = across(embeddings, 1)
    near_other = across(near, 1)
    near_second_other = [across(f, 1) for f in near_second]
    near_first_other = [across(f, 1) for f in near_first]
    first_far_other = [across(f, 1) for f in first_far]
    rest_far_other = [(across(f[:TILE], 1), across(f[TILE:], 1)) for f in rest_far]
    seeds_other = across(after(seeds, (near_other, near_second_other)), 1)

    arrays = []
    windows = {"x": [], "mine": [], "other": []}

    def place(*blocks):
        out = []
        for block, tiles in blocks:
            at = [i for i, a in enumerate(arrays) if a is block]
            if not at:
                arrays.append(block)
                at = [len(arrays) - 1]
            out += [(at[0], t * TILE) for t in tiles]
        return out

    own, more = range(groups), range(groups - 1)
    windows["x"].append(place((embeddings, own), (near, range(SPILL))))
    windows["x"].append(place((own_other, own), (near_other, range(SPILL))))
    for m in range(half - 1):
        windows["x"].append(
            place((first_far[m], [0]), (rest_far[m], more), (near_first[m], [0]), (near_second[m], [0]))
        )
        one, others = rest_far_other[m]
        windows["x"].append(
            place(
                (first_far_other[m], [0]), (one, [0]), (others, range(groups - 2)),
                (near_first_other[m], [0]), (near_second_other[m], [0]),
            )
        )
    windows["mine"] += place((seeds, [0]))
    windows["other"] += place((seeds_other, [0]))
    for m in range(half - 1):
        if packed:
            windows["mine"] += place((first_far[m], [1]))
            windows["other"] += place((first_far_other[m], [1]))
        else:
            windows["mine"] += place((seeds_far[m], [0]))
            windows["other"] += place((across(seeds_far[m], 1), [0]))
    if packed:
        windows["mine"] += place((near_first[0], [1]))
        windows["other"] += place((near_first_other[0], [1]))
    else:
        windows["mine"] += place((near_seeds, [0]))
        windows["other"] += place((across(near_seeds, 1), [0]))

    smem = pl.BlockSpec(memory_space=pltpu.SMEM)
    vmem = pl.BlockSpec(memory_space=pltpu.VMEM)
    params = pltpu.CompilerParams(vmem_limit_bytes=40 * 1024 * 1024)
    little = pl.CostEstimate(flops=1, bytes_accessed=1, transcendentals=0)
    labels_shape = jax.ShapeDtypeStruct((TILE, concepts), jnp.bfloat16)
    codes = pl.pallas_call(
        functools.partial(code_kernel, groups),
        out_shape=(
            jax.ShapeDtypeStruct((half * 8, wtiles * TILE), jnp.float32),
            jax.ShapeDtypeStruct((half * 8, wtiles * TILE), jnp.float32),
            jax.ShapeDtypeStruct((half * TILE, 128), jnp.float32),
        ),
        in_specs=[smem, smem, vmem, vmem],
        out_specs=(vmem, vmem, vmem),
        compiler_params=params,
        cost_estimate=little,
        name="codes",
    )(blocks, counts, clusters.reshape(1, -1), near)

    def affinity_of(m):
        return pl.pallas_call(
            functools.partial(affinity_kernel, groups, m, windows),
            out_shape=(jax.ShapeDtypeStruct((wtiles, TILE, TILE), jnp.bfloat16), labels_shape),
            in_specs=[vmem] * (3 + len(arrays)),
            out_specs=(vmem, vmem),
            scratch_shapes=[pltpu.VMEM((wtiles, TILE, TILE), jnp.float32)],
            compiler_params=params,
            cost_estimate=little,
            name=f"affinity_{m}",
        )(*codes, *arrays)

    affinity, labels = zip(*[affinity_of(m) for m in range(half)])
    labels = list(labels) + [from_next(labels[0])]
    others = [across(l, 1) for l in labels]
    return pl.pallas_call(
        functools.partial(last_kernel, groups),
        out_shape=labels_shape,
        in_specs=[vmem] * (1 + half + 2 * len(labels)),
        out_specs=vmem,
        compiler_params=params,
        name="spread_last",
    )(seeds, *affinity, *labels, *others)


def solution(mesh):
    in_specs = (
        P("shard", "grp"),
        P("shard"),
        P("shard", None),
        P("shard"),
        P(("shard", "grp")),
        P(("shard", "grp"), None),
    )
    out_specs = P(("shard", "grp"), None)
    return jax.shard_map(local, mesh=mesh, in_specs=in_specs, out_specs=out_specs, check_vma=False)
```

```python
import functools

import jax
import jax.numpy as jnp
from jax import lax
from jax.experimental import pallas as pl
from jax.experimental.pallas import tpu as pltpu
from jax.sharding import PartitionSpec as P

TILE = 256
K = 4
SPILL = 2
ROWS = 32

kernel_width = 0.06
spread_weight = 0.6
MASKED = -1e30
SCALE = 1.4426950408889634 / kernel_width

NT = (((1,), (1,)), ((), ()))


def across(block, distance):
    groups = lax.axis_size("grp")
    return lax.ppermute(block, "grp", [(i, i ^ distance) for i in range(groups)])


def from_next(block):
    shards = lax.axis_size("shard")
    return lax.ppermute(block, "shard", [(i + 1, i) for i in range(shards - 1)])


def bundle(*blocks):
    if len({b.shape[1] for b in blocks}) == 1:
        return (jnp.concatenate(blocks),)
    return blocks


def tile_in(blocks, t):
    return blocks[0][t * TILE:(t + 1) * TILE] if len(blocks) == 1 else blocks[t]


def masked(mask, labels):
    return jnp.where(mask[:, None] > 0, labels, jnp.zeros_like(labels))


def after(block, done):
    return lax.optimization_barrier((block, done))[0]


def listed(blocks_ref, counts_ref, tile, groups):
    base = lax.axis_index("shard") * groups
    count = counts_ref[tile]
    ids = [blocks_ref[tile, k] - base for k in range(K)]
    return [
        sum(jnp.where((ids[k] == w) & (k < count), 1, 0) for k in range(K))
        for w in range(groups + SPILL)
    ]


def squares(tiles):
    return functools.reduce(
        jnp.add,
        [
            jnp.square(t[:, h * 128:(h + 1) * 128].astype(jnp.float32))
            for t in tiles
            for h in range(t.shape[1] // 128)
        ],
    )


def row_norms(tiles):
    return jnp.sum(squares(tiles), axis=1, keepdims=True) * SCALE


def column_terms(rows, tiles):
    dots = functools.reduce(
        jnp.add,
        [
            lax.dot_general(r, t, NT, preferred_element_type=jnp.float32)
            for r, t in zip(rows, tiles)
        ],
    )
    return dots * (2.0 * SCALE) - jnp.sum(squares(tiles).T, axis=0, keepdims=True) * SCALE


def early_kernel(
    groups, m, blocks_ref, counts_ref, clusters_ref, own_ref, other_ref, part_ref, factor_ref,
    row_ref,
):
    core = lax.rem(lax.axis_index("grp"), 2)
    eye = lax.broadcasted_iota(jnp.int32, (TILE, TILE), 0) == lax.broadcasted_iota(
        jnp.int32, (TILE, TILE), 1
    )
    tile = 2 * m + core
    at = pl.ds(pl.multiple_of(tile * TILE, TILE), TILE)
    rows = [own_ref[at, :], other_ref[at, :]]
    norms = row_norms(rows)
    own = clusters_ref[:, at].astype(jnp.float32)
    own = jnp.sum(jnp.where(eye, own, jnp.zeros_like(own)), axis=1, keepdims=True)
    row_ref[:, :128] = jnp.broadcast_to(own, (TILE, 128))
    row_ref[:, 128:] = jnp.broadcast_to(norms, (TILE, 128))
    for w, mult in enumerate(listed(blocks_ref, counts_ref, tile, groups)):
        columns = slice(w * TILE, (w + 1) * TILE)
        factor = jnp.full((1, TILE), mult.astype(jnp.float32))
        factor_ref[:, columns] = jnp.broadcast_to(factor, (8, TILE))
        if w < groups:
            cluster = clusters_ref[:, columns].astype(jnp.float32)
            allowed = own == jnp.where(factor > 0, cluster, -1.0)
            if w // 2 == m:
                allowed = allowed & jnp.logical_not(eye & (tile == w))
            terms = column_terms(rows, [own_ref[columns, :], other_ref[columns, :]])
            part_ref[w] = jnp.where(allowed, terms - norms, MASKED)


def rows_of(columns, m, quarters):
    core = lax.rem(lax.axis_index("grp"), 2)
    return [jnp.where(core == 0, columns(2 * m, q), columns(2 * m + 1, q)) for q in quarters]


def logit_kernel(
    groups, m, windows, part_ref, factor_ref, row_ref, own_ref, other_ref, near_ref,
    near_other_ref, *refs,
):
    ins, logit_ref = refs[:-1], refs[-1]
    quarters = range(2, groups)
    core = lax.rem(lax.axis_index("grp"), 2)

    def columns(w, q):
        ref, row = windows[q][w]
        return ins[ref][row:row + TILE, :]

    rows = rows_of(columns, m, quarters)
    norms = row_norms(rows)
    for w in range(groups):
        logit_ref[w] = (
            part_ref[w] - norms + column_terms(rows, [columns(w, q) for q in quarters])
        )
    at = pl.ds(pl.multiple_of((2 * m + core) * TILE, TILE), TILE)
    rows = [own_ref[at, :], other_ref[at, :]] + rows
    norms = norms + row_ref[:, 128:129]
    packed = near_ref[SPILL * TILE:, :].astype(jnp.float32)
    width = packed.shape[1]
    for t in range(SPILL):
        w = groups + t
        cluster = jnp.concatenate(
            [packed[i // width:i // width + 1, :] for i in range(t * TILE, (t + 1) * TILE, width)],
            axis=1,
        )
        factor = factor_ref[0:1, w * TILE:(w + 1) * TILE]
        allowed = row_ref[:, 0:1] == jnp.where(factor > 0, cluster, -1.0)
        tiles = [ref[t * TILE:(t + 1) * TILE, :] for ref in (near_ref, near_other_ref)]
        if t:
            tiles += [columns(w, q) for q in quarters]
        logit_ref[w] = jnp.where(allowed, column_terms(rows, tiles) - norms, MASKED)


def spread(aff_ref, parts, seed):
    total = jnp.zeros(seed.shape, jnp.float32)
    for w, ref in parts:
        total += jnp.dot(aff_ref[w], ref[...], preferred_element_type=jnp.float32)
    return (spread_weight * total + (1.0 - spread_weight) * seed.astype(jnp.float32)).astype(
        jnp.bfloat16
    )


def affinity_kernel(groups, m, windows, logit_ref, factor_ref, *refs):
    half = groups // 2
    wtiles = groups + SPILL
    ins, (aff_ref, labels_ref, late_ref) = refs[:-3], refs[-3:]
    member = lax.axis_index("grp")
    core = lax.rem(member, 2)
    pair = member // 2
    quarters = range(2, groups)

    def piece(at):
        ref, row = at
        return ins[ref].at[row:row + TILE, :]

    def columns(w, q):
        return piece(windows["x"][q][w])[...]

    late_ref[...] = logit_ref[groups] + column_terms(
        rows_of(columns, m, quarters), [columns(groups, q) for q in quarters]
    )

    def softmax(step, carry):
        at = pl.ds(pl.multiple_of(step * ROWS, ROWS), ROWS)
        logits = [logit_ref[w, at, :] for w in range(wtiles)]
        logits[groups] = late_ref[at, :]
        top = jnp.max(functools.reduce(jnp.maximum, logits), axis=1, keepdims=True)
        weights = [
            jnp.exp2(logits[w] - top) * factor_ref[0:1, w * TILE:(w + 1) * TILE]
            for w in range(wtiles)
        ]
        total = jnp.sum(functools.reduce(jnp.add, weights), axis=1, keepdims=True)
        share = 1.0 / total
        for w in range(wtiles):
            aff_ref[w, at, :] = (weights[w] * share).astype(jnp.bfloat16)
        return carry

    lax.fori_loop(0, TILE // ROWS, softmax, 0, unroll=True)

    parts = []
    for r in range(half):
        parts.append((2 * (pair ^ r) + core, piece(windows["mine"][r])))
        parts.append((2 * (pair ^ r) + 1 - core, piece(windows["other"][r])))
    parts.append((groups + core, piece(windows["mine"][half])))
    parts.append((groups + 1 - core, piece(windows["other"][half])))
    seed = piece(windows["mine"][0])[...]
    for r in range(1, half):
        seed = jnp.where((pair ^ m) == r, piece(windows["mine"][r])[...], seed)
    labels_ref[...] = spread(aff_ref, parts, seed)


def own_kernel(groups, seed_ref, *refs):
    half = groups // 2
    core = lax.rem(lax.axis_index("grp"), 2)
    affs, mine, other, out_ref = refs[:half], refs[half:2 * half], refs[2 * half:3 * half], refs[-1]
    for p in range(half):
        @pl.when(lax.axis_index("grp") // 2 == p)
        def _(p=p):
            total = jnp.zeros(out_ref.shape, jnp.float32)
            for m in range(half):
                for w, ref in ((2 * m + core, mine[m]), (2 * m + 1 - core, other[m])):
                    total += jnp.dot(affs[p][w], ref[...], preferred_element_type=jnp.float32)
            out_ref[...] = spread_weight * total + (1.0 - spread_weight) * seed_ref[...].astype(
                jnp.float32
            )


def near_kernel(groups, distance, total_ref, labels_ref, *refs):
    affs, out_ref = refs[:-1], refs[-1]
    core = lax.rem(lax.axis_index("grp"), 2)
    for p in range(groups // 2):
        @pl.when(lax.axis_index("grp") // 2 == p)
        def _(p=p):
            out_ref[...] = (
                total_ref[...]
                + spread_weight
                * jnp.dot(
                    affs[p][groups + (core ^ distance)], labels_ref[...],
                    preferred_element_type=jnp.float32,
                )
            ).astype(out_ref.dtype)


def local(embeddings, clusters, blocks, counts, seed_mask, prior):
    groups = lax.axis_size("grp")
    half = groups // 2
    apart = range(1, half)
    pair = lax.axis_index("grp") // 2
    width = embeddings.shape[1]
    concepts = prior.shape[1]
    wtiles = groups + SPILL
    head_rows = SPILL * TILE
    smem = pl.BlockSpec(memory_space=pltpu.SMEM)
    vmem = pl.BlockSpec(memory_space=pltpu.VMEM)
    params = pltpu.CompilerParams(vmem_limit_bytes=40 * 1024 * 1024)
    little = pl.CostEstimate(flops=1, bytes_accessed=1, transcendentals=0)
    labels_shape = jax.ShapeDtypeStruct((TILE, concepts), jnp.bfloat16)

    first_far = [
        tuple(across(b, 2 * m) for b in bundle(embeddings[:TILE], prior)) for m in apart
    ]
    mask_far = [across(seed_mask, 2 * m) for m in apart]
    rest_far = [across(embeddings[TILE:], 2 * m) for m in apart]

    head_c = clusters[:head_rows].astype(jnp.bfloat16).reshape(-1, width)
    head_c = jnp.pad(head_c, ((0, 16 - head_c.shape[0]), (0, 0)))
    near = from_next(jnp.concatenate([embeddings[:head_rows], head_c]))

    own_other = across(embeddings, 1)
    near_other = across(near, 1)

    def early_of(m, done=()):
        own, other = after((embeddings, own_other), done) if m else (embeddings, own_other)
        return pl.pallas_call(
            functools.partial(early_kernel, groups, m),
            out_shape=(
                jax.ShapeDtypeStruct((groups, TILE, TILE), jnp.float32),
                jax.ShapeDtypeStruct((8, wtiles * TILE), jnp.float32),
                jax.ShapeDtypeStruct((TILE, 256), jnp.float32),
            ),
            in_specs=[smem, smem] + [vmem] * 3,
            out_specs=(vmem, vmem, vmem),
            compiler_params=params,
            cost_estimate=little,
            name=f"early_{m}",
        )(blocks, counts, clusters.reshape(1, -1), own, other)

    first_early = early_of(0)

    seeds = masked(seed_mask, prior)
    seeds_far = [masked(k, tile_in(f, 1)) for k, f in zip(mask_far, first_far)]
    head_seeds = seeds
    for m in apart:
        head_seeds = jnp.where(pair == m, seeds_far[m - 1], head_seeds)
    first_on = [bundle(tile_in(first_far[0], 0), head_seeds)]
    first_on += [(tile_in(f, 0),) for f in first_far[1:]]
    first_on = after(first_on, first_early)
    near_first = [tuple(from_next(b) for b in f) for f in first_on]

    near_second = [across(near[TILE:head_rows], 2 * m) for m in apart]

    near_second_other = [across(f, 1) for f in near_second]
    near_first_other = [tuple(across(b, 1) for b in f) for f in near_first]
    first_far_other = [across(tile_in(f, 0), 1) for f in first_far]
    rest_far_other = [(across(f[:TILE], 1), across(f[TILE:], 1)) for f in rest_far]
    seeds_other = across(seeds, 1)
    seeds_far_other = [across(f, 1) for f in seeds_far]

    arrays = []

    def place(*blocks):
        out = []
        for block, tiles in blocks:
            at = [i for i, a in enumerate(arrays) if a is block]
            if not at:
                arrays.append(block)
                at = [len(arrays) - 1]
            out += [(at[0], t * TILE) for t in tiles]
        return out

    def seeds_in(f):
        return (f[0], [1]) if len(f) == 1 else (f[1], [0])

    windows = {"x": [None, None], "mine": place((seeds, [0])), "other": place((seeds_other, [0]))}
    for m in range(half - 1):
        windows["x"].append(
            place(
                (first_far[m][0], [0]), (rest_far[m], range(groups - 1)),
                (near_first[m][0], [0]), (near_second[m], [0]),
            )
        )
        one, more = rest_far_other[m]
        windows["x"].append(
            place(
                (first_far_other[m], [0]), (one, [0]), (more, range(groups - 2)),
                (near_first_other[m][0], [0]), (near_second_other[m], [0]),
            )
        )
        windows["mine"] += place((seeds_far[m], [0]))
        windows["other"] += place((seeds_far_other[m], [0]))
    windows["mine"] += place(seeds_in(near_first[0]))
    windows["other"] += place(seeds_in(near_first_other[0]))

    early_arrays = []
    early_windows = [None, None]
    for q in range(2, groups):
        tiles = []
        for w, (ref, row) in enumerate(windows["x"][q]):
            if w == groups:
                tiles.append(None)
                continue
            at = [i for i, a in enumerate(early_arrays) if a is arrays[ref]]
            if not at:
                early_arrays.append(arrays[ref])
                at = [len(early_arrays) - 1]
            tiles.append((at[0], row))
        early_windows.append(tiles)

    def affinity_of(m, done):
        early = early_of(m, done) if m else first_early
        logits = pl.pallas_call(
            functools.partial(logit_kernel, groups, m, early_windows),
            out_shape=jax.ShapeDtypeStruct((wtiles, TILE, TILE), jnp.float32),
            in_specs=[vmem] * (7 + len(early_arrays)),
            out_specs=vmem,
            compiler_params=params,
            cost_estimate=little,
            name=f"logits_{m}",
        )(*early, embeddings, own_other, near, near_other, *early_arrays)
        return pl.pallas_call(
            functools.partial(affinity_kernel, groups, m, windows),
            out_shape=(jax.ShapeDtypeStruct((wtiles, TILE, TILE), jnp.bfloat16), labels_shape),
            in_specs=[vmem] * (2 + len(arrays)),
            out_specs=(vmem, vmem),
            scratch_shapes=[pltpu.VMEM((TILE, TILE), jnp.float32)],
            compiler_params=params,
            cost_estimate=little,
            name=f"affinity_{m}",
        )(logits, early[1], *arrays)

    affinity, labels = [], []
    for m in range(half):
        a, l = affinity_of(m, labels[-1:])
        affinity.append(a)
        labels.append(l)
    near_labels = from_next(labels[0])
    near_labels_other = across(near_labels, 1)
    others = [across(l, 1) for l in labels]
    total = pl.pallas_call(
        functools.partial(own_kernel, groups),
        out_shape=jax.ShapeDtypeStruct((TILE, concepts), jnp.float32),
        in_specs=[vmem] * (1 + 3 * half),
        out_specs=vmem,
        compiler_params=params,
        cost_estimate=little,
        name="spread_own",
    )(seeds, *affinity, *labels, *others)
    for distance, block in enumerate((near_labels, near_labels_other)):
        total = pl.pallas_call(
            functools.partial(near_kernel, groups, distance),
            out_shape=jax.ShapeDtypeStruct((TILE, concepts), jnp.bfloat16 if distance else jnp.float32),
            in_specs=[vmem] * (2 + half),
            out_specs=vmem,
            compiler_params=params,
            cost_estimate=little,
            name=f"spread_near_{distance}",
        )(total, block, *affinity)
    return total


def solution(mesh):
    in_specs = (
        P("shard", "grp"),
        P("shard"),
        P("shard", None),
        P("shard"),
        P(("shard", "grp")),
        P(("shard", "grp"), None),
    )
    out_specs = P(("shard", "grp"), None)
    return jax.shard_map(local, mesh=mesh, in_specs=in_specs, out_specs=out_specs, check_vma=False)
```

```python
import functools

import jax
import jax.numpy as jnp
from jax import lax
from jax.experimental import pallas as pl
from jax.experimental.pallas import tpu as pltpu
from jax.sharding import PartitionSpec as P

TILE = 256
K = 4
SPILL = 2
ROWS = 32

kernel_width = 0.06
spread_weight = 0.6
MASKED = -1e30
SCALE = 1.4426950408889634 / kernel_width

NT = (((1,), (1,)), ((), ()))


def across(block, distance):
    groups = lax.axis_size("grp")
    return lax.ppermute(block, "grp", [(i, i ^ distance) for i in range(groups)])


def from_next(block):
    shards = lax.axis_size("shard")
    return lax.ppermute(block, "shard", [(i + 1, i) for i in range(shards - 1)])


def bundle(*blocks):
    if len({b.shape[1] for b in blocks}) == 1:
        return (jnp.concatenate(blocks),)
    return blocks


def tile_and(tiles, block):
    if tiles.shape[1] != block.shape[1]:
        return tiles[:TILE], block
    first = lax.broadcasted_iota(jnp.int32, tiles.shape, 0) < TILE
    return (jnp.where(first, tiles, jnp.concatenate([block, block])),)


def tile_in(blocks, t):
    return blocks[0][t * TILE:(t + 1) * TILE] if len(blocks) == 1 else blocks[t]


def masked(mask, labels):
    return jnp.where(mask[:, None] > 0, labels, jnp.zeros_like(labels))


def after(block, done):
    return lax.optimization_barrier((block, done))[0]


def listed(blocks_ref, counts_ref, tile, groups):
    base = lax.axis_index("shard") * groups
    count = counts_ref[tile]
    ids = [blocks_ref[tile, k] - base for k in range(K)]
    return [
        sum(jnp.where((ids[k] == w) & (k < count), 1, 0) for k in range(K))
        for w in range(groups + SPILL)
    ]


def squares(tiles):
    return functools.reduce(
        jnp.add,
        [
            jnp.square(t[:, h * 128:(h + 1) * 128].astype(jnp.float32))
            for t in tiles
            for h in range(t.shape[1] // 128)
        ],
    )


def row_norms(tiles):
    return jnp.sum(squares(tiles), axis=1, keepdims=True) * SCALE


def column_terms(rows, tiles):
    dots = functools.reduce(
        jnp.add,
        [
            lax.dot_general(r, t, NT, preferred_element_type=jnp.float32)
            for r, t in zip(rows, tiles)
        ],
    )
    return dots * (2.0 * SCALE) - jnp.sum(squares(tiles).T, axis=0, keepdims=True) * SCALE


def early_kernel(
    groups, m, blocks_ref, counts_ref, clusters_ref, own_ref, other_ref, part_ref, factor_ref,
    row_ref,
):
    core = lax.rem(lax.axis_index("grp"), 2)
    eye = lax.broadcasted_iota(jnp.int32, (TILE, TILE), 0) == lax.broadcasted_iota(
        jnp.int32, (TILE, TILE), 1
    )
    tile = 2 * m + core
    at = pl.ds(pl.multiple_of(tile * TILE, TILE), TILE)
    rows = [own_ref[at, :], other_ref[at, :]]
    norms = row_norms(rows)
    own = clusters_ref[:, at].astype(jnp.float32)
    own = jnp.sum(jnp.where(eye, own, jnp.zeros_like(own)), axis=1, keepdims=True)
    row_ref[:, :128] = jnp.broadcast_to(own, (TILE, 128))
    row_ref[:, 128:] = jnp.broadcast_to(norms, (TILE, 128))
    for w, mult in enumerate(listed(blocks_ref, counts_ref, tile, groups)):
        columns = slice(w * TILE, (w + 1) * TILE)
        factor = jnp.full((1, TILE), mult.astype(jnp.float32))
        factor_ref[:, columns] = jnp.broadcast_to(factor, (8, TILE))
        if w < groups:
            cluster = clusters_ref[:, columns].astype(jnp.float32)
            allowed = own == jnp.where(factor > 0, cluster, -1.0)
            if w // 2 == m:
                allowed = allowed & jnp.logical_not(eye & (tile == w))
            terms = column_terms(rows, [own_ref[columns, :], other_ref[columns, :]])
            part_ref[w] = jnp.where(allowed, terms - norms, MASKED)


def rows_of(columns, m, quarters):
    core = lax.rem(lax.axis_index("grp"), 2)
    return [jnp.where(core == 0, columns(2 * m, q), columns(2 * m + 1, q)) for q in quarters]


def logit_kernel(
    groups, m, windows, part_ref, factor_ref, row_ref, own_ref, other_ref, near_ref,
    near_other_ref, *refs,
):
    ins, logit_ref = refs[:-1], refs[-1]
    quarters = range(2, groups)
    core = lax.rem(lax.axis_index("grp"), 2)

    def columns(w, q):
        ref, row = windows[q][w]
        return ins[ref][row:row + TILE, :]

    rows = rows_of(columns, m, quarters)
    norms = row_norms(rows)
    for w in range(groups):
        logit_ref[w] = (
            part_ref[w] - norms + column_terms(rows, [columns(w, q) for q in quarters])
        )
    at = pl.ds(pl.multiple_of((2 * m + core) * TILE, TILE), TILE)
    rows = [own_ref[at, :], other_ref[at, :]] + rows
    norms = norms + row_ref[:, 128:129]
    packed = near_ref[SPILL * TILE:, :].astype(jnp.float32)
    width = packed.shape[1]
    for t in range(SPILL):
        w = groups + t
        cluster = jnp.concatenate(
            [packed[i // width:i // width + 1, :] for i in range(t * TILE, (t + 1) * TILE, width)],
            axis=1,
        )
        factor = factor_ref[0:1, w * TILE:(w + 1) * TILE]
        allowed = row_ref[:, 0:1] == jnp.where(factor > 0, cluster, -1.0)
        tiles = [ref[t * TILE:(t + 1) * TILE, :] for ref in (near_ref, near_other_ref)]
        if t:
            tiles += [columns(w, q) for q in quarters]
        logit_ref[w] = jnp.where(allowed, column_terms(rows, tiles) - norms, MASKED)


def spread(aff_ref, parts, seed):
    total = jnp.zeros(seed.shape, jnp.float32)
    for w, ref in parts:
        total += jnp.dot(aff_ref[w], ref[...], preferred_element_type=jnp.float32)
    return (spread_weight * total + (1.0 - spread_weight) * seed.astype(jnp.float32)).astype(
        jnp.bfloat16
    )


def affinity_kernel(groups, m, windows, logit_ref, factor_ref, *refs):
    half = groups // 2
    wtiles = groups + SPILL
    ins, (aff_ref, labels_ref, late_ref) = refs[:-3], refs[-3:]
    member = lax.axis_index("grp")
    core = lax.rem(member, 2)
    pair = member // 2
    quarters = range(2, groups)

    def piece(at):
        ref, row = at
        return ins[ref].at[row:row + TILE, :]

    def columns(w, q):
        return piece(windows["x"][q][w])[...]

    late_ref[...] = logit_ref[groups] + column_terms(
        rows_of(columns, m, quarters), [columns(groups, q) for q in quarters]
    )

    def softmax(step, carry):
        at = pl.ds(pl.multiple_of(step * ROWS, ROWS), ROWS)
        logits = [logit_ref[w, at, :] for w in range(wtiles)]
        logits[groups] = late_ref[at, :]
        top = jnp.max(functools.reduce(jnp.maximum, logits), axis=1, keepdims=True)
        weights = [
            jnp.exp2(logits[w] - top) * factor_ref[0:1, w * TILE:(w + 1) * TILE]
            for w in range(wtiles)
        ]
        total = jnp.sum(functools.reduce(jnp.add, weights), axis=1, keepdims=True)
        share = 1.0 / total
        for w in range(wtiles):
            aff_ref[w, at, :] = (weights[w] * share).astype(jnp.bfloat16)
        return carry

    lax.fori_loop(0, TILE // ROWS, softmax, 0, unroll=True)

    parts = []
    for r in range(half):
        parts.append((2 * (pair ^ r) + core, piece(windows["mine"][r])))
        parts.append((2 * (pair ^ r) + 1 - core, piece(windows["other"][r])))
    parts.append((groups + core, piece(windows["mine"][half])))
    parts.append((groups + 1 - core, piece(windows["other"][half])))
    seed = piece(windows["mine"][0])[...]
    for r in range(1, half):
        seed = jnp.where((pair ^ m) == r, piece(windows["mine"][r])[...], seed)
    labels_ref[...] = spread(aff_ref, parts, seed)


def own_kernel(groups, seed_ref, *refs):
    half = groups // 2
    core = lax.rem(lax.axis_index("grp"), 2)
    affs, mine, other, out_ref = refs[:half], refs[half:2 * half], refs[2 * half:3 * half], refs[-1]
    for p in range(half):
        @pl.when(lax.axis_index("grp") // 2 == p)
        def _(p=p):
            total = jnp.zeros(out_ref.shape, jnp.float32)
            for m in range(half):
                for w, ref in ((2 * m + core, mine[m]), (2 * m + 1 - core, other[m])):
                    total += jnp.dot(affs[p][w], ref[...], preferred_element_type=jnp.float32)
            out_ref[...] = spread_weight * total + (1.0 - spread_weight) * seed_ref[...].astype(
                jnp.float32
            )


def near_kernel(groups, distance, total_ref, labels_ref, *refs):
    affs, out_ref = refs[:-1], refs[-1]
    core = lax.rem(lax.axis_index("grp"), 2)
    for p in range(groups // 2):
        @pl.when(lax.axis_index("grp") // 2 == p)
        def _(p=p):
            out_ref[...] = (
                total_ref[...]
                + spread_weight
                * jnp.dot(
                    affs[p][groups + (core ^ distance)], labels_ref[...],
                    preferred_element_type=jnp.float32,
                )
            ).astype(out_ref.dtype)


def local(embeddings, clusters, blocks, counts, seed_mask, prior):
    groups = lax.axis_size("grp")
    half = groups // 2
    apart = range(1, half)
    pair = lax.axis_index("grp") // 2
    width = embeddings.shape[1]
    concepts = prior.shape[1]
    wtiles = groups + SPILL
    head_rows = SPILL * TILE
    smem = pl.BlockSpec(memory_space=pltpu.SMEM)
    vmem = pl.BlockSpec(memory_space=pltpu.VMEM)
    params = pltpu.CompilerParams(vmem_limit_bytes=40 * 1024 * 1024)
    little = pl.CostEstimate(flops=1, bytes_accessed=1, transcendentals=0)
    labels_shape = jax.ShapeDtypeStruct((TILE, concepts), jnp.bfloat16)

    first_far = [
        tuple(across(b, 2 * m) for b in tile_and(embeddings[:2 * TILE], prior)) for m in apart
    ]
    mask_far = [across(seed_mask, 2 * m) for m in apart]
    rest_far = [across(embeddings[TILE:], 2 * m) for m in apart]

    head_c = clusters[:head_rows].astype(jnp.bfloat16).reshape(-1, width)
    head_c = jnp.pad(head_c, ((0, 16 - head_c.shape[0]), (0, 0)))
    near = from_next(jnp.concatenate([embeddings[:head_rows], head_c]))

    own_other = across(embeddings, 1)
    near_other = across(near, 1)

    def early_of(m, done=()):
        own, other = after((embeddings, own_other), done) if m else (embeddings, own_other)
        return pl.pallas_call(
            functools.partial(early_kernel, groups, m),
            out_shape=(
                jax.ShapeDtypeStruct((groups, TILE, TILE), jnp.float32),
                jax.ShapeDtypeStruct((8, wtiles * TILE), jnp.float32),
                jax.ShapeDtypeStruct((TILE, 256), jnp.float32),
            ),
            in_specs=[smem, smem] + [vmem] * 3,
            out_specs=(vmem, vmem, vmem),
            compiler_params=params,
            cost_estimate=little,
            name=f"early_{m}",
        )(blocks, counts, clusters.reshape(1, -1), own, other)

    first_early = early_of(0)

    seeds = masked(seed_mask, prior)
    seeds_far = [masked(k, tile_in(f, 1)) for k, f in zip(mask_far, first_far)]
    head_seeds = seeds
    for m in apart:
        head_seeds = jnp.where(pair == m, seeds_far[m - 1], head_seeds)
    first_on = [bundle(tile_in(first_far[0], 0), head_seeds)]
    first_on += [(tile_in(f, 0),) for f in first_far[1:]]
    first_on = after(first_on, first_early)
    near_first = [tuple(from_next(b) for b in f) for f in first_on]

    near_second = [across(near[TILE:head_rows], 2 * m) for m in apart]

    near_second_other = [across(f, 1) for f in near_second]
    near_first_other = [tuple(across(b, 1) for b in f) for f in near_first]
    first_far_other = [across(tile_in(f, 0), 1) for f in first_far]
    rest_far_other = [(across(f[:TILE], 1), across(f[TILE:], 1)) for f in rest_far]
    seeds_other = across(seeds, 1)
    seeds_far_other = [across(f, 1) for f in seeds_far]

    arrays = []

    def place(*blocks):
        out = []
        for block, tiles in blocks:
            at = [i for i, a in enumerate(arrays) if a is block]
            if not at:
                arrays.append(block)
                at = [len(arrays) - 1]
            out += [(at[0], t * TILE) for t in tiles]
        return out

    def seeds_in(f):
        return (f[0], [1]) if len(f) == 1 else (f[1], [0])

    windows = {"x": [None, None], "mine": place((seeds, [0])), "other": place((seeds_other, [0]))}
    for m in range(half - 1):
        windows["x"].append(
            place(
                (first_far[m][0], [0]), (rest_far[m], range(groups - 1)),
                (near_first[m][0], [0]), (near_second[m], [0]),
            )
        )
        one, more = rest_far_other[m]
        windows["x"].append(
            place(
                (first_far_other[m], [0]), (one, [0]), (more, range(groups - 2)),
                (near_first_other[m][0], [0]), (near_second_other[m], [0]),
            )
        )
        windows["mine"] += place((seeds_far[m], [0]))
        windows["other"] += place((seeds_far_other[m], [0]))
    windows["mine"] += place(seeds_in(near_first[0]))
    windows["other"] += place(seeds_in(near_first_other[0]))

    early_arrays = []
    early_windows = [None, None]
    for q in range(2, groups):
        tiles = []
        for w, (ref, row) in enumerate(windows["x"][q]):
            if w == groups:
                tiles.append(None)
                continue
            at = [i for i, a in enumerate(early_arrays) if a is arrays[ref]]
            if not at:
                early_arrays.append(arrays[ref])
                at = [len(early_arrays) - 1]
            tiles.append((at[0], row))
        early_windows.append(tiles)

    def affinity_of(m, done):
        early = early_of(m, done) if m else first_early
        logits = pl.pallas_call(
            functools.partial(logit_kernel, groups, m, early_windows),
            out_shape=jax.ShapeDtypeStruct((wtiles, TILE, TILE), jnp.float32),
            in_specs=[vmem] * (7 + len(early_arrays)),
            out_specs=vmem,
            compiler_params=params,
            cost_estimate=little,
            name=f"logits_{m}",
        )(*early, embeddings, own_other, near, near_other, *early_arrays)
        return pl.pallas_call(
            functools.partial(affinity_kernel, groups, m, windows),
            out_shape=(jax.ShapeDtypeStruct((wtiles, TILE, TILE), jnp.bfloat16), labels_shape),
            in_specs=[vmem] * (2 + len(arrays)),
            out_specs=(vmem, vmem),
            scratch_shapes=[pltpu.VMEM((TILE, TILE), jnp.float32)],
            compiler_params=params,
            cost_estimate=little,
            name=f"affinity_{m}",
        )(logits, early[1], *arrays)

    affinity, labels = [], []
    for m in range(half):
        a, l = affinity_of(m, labels[-1:])
        affinity.append(a)
        labels.append(l)
    near_labels = from_next(labels[0])
    near_labels_other = across(near_labels, 1)
    others = [across(l, 1) for l in labels]
    total = pl.pallas_call(
        functools.partial(own_kernel, groups),
        out_shape=jax.ShapeDtypeStruct((TILE, concepts), jnp.float32),
        in_specs=[vmem] * (1 + 3 * half),
        out_specs=vmem,
        compiler_params=params,
        cost_estimate=little,
        name="spread_own",
    )(seeds, *affinity, *labels, *others)
    for distance, block in enumerate((near_labels, near_labels_other)):
        total = pl.pallas_call(
            functools.partial(near_kernel, groups, distance),
            out_shape=jax.ShapeDtypeStruct((TILE, concepts), jnp.bfloat16 if distance else jnp.float32),
            in_specs=[vmem] * (2 + half),
            out_specs=vmem,
            compiler_params=params,
            cost_estimate=little,
            name=f"spread_near_{distance}",
        )(total, block, *affinity)
    return total


def solution(mesh):
    in_specs = (
        P("shard", "grp"),
        P("shard"),
        P("shard", None),
        P("shard"),
        P(("shard", "grp")),
        P(("shard", "grp"), None),
    )
    out_specs = P(("shard", "grp"), None)
    return jax.shard_map(local, mesh=mesh, in_specs=in_specs, out_specs=out_specs, check_vma=False)
```

```python
import functools

import jax
import jax.numpy as jnp
from jax import lax
from jax.experimental import pallas as pl
from jax.experimental.pallas import tpu as pltpu
from jax.sharding import PartitionSpec as P

TILE = 256
K = 4
SPILL = 2
ROWS = 32

kernel_width = 0.06
spread_weight = 0.6
MASKED = -1e30
SCALE = 1.4426950408889634 / kernel_width

NT = (((1,), (1,)), ((), ()))


def across(block, distance):
    groups = lax.axis_size("grp")
    return lax.ppermute(block, "grp", [(i, i ^ distance) for i in range(groups)])


def from_next(block):
    shards = lax.axis_size("shard")
    return lax.ppermute(block, "shard", [(i + 1, i) for i in range(shards - 1)])


def bundle(*blocks):
    if len({b.shape[1] for b in blocks}) == 1:
        return (jnp.concatenate(blocks),)
    return blocks


def tile_and(tiles, block):
    if tiles.shape[1] != block.shape[1]:
        return tiles[:TILE], block
    first = lax.broadcasted_iota(jnp.int32, tiles.shape, 0) < TILE
    return (jnp.where(first, tiles, jnp.concatenate([block, block])),)


def tile_in(blocks, t):
    return blocks[0][t * TILE:(t + 1) * TILE] if len(blocks) == 1 else blocks[t]


def masked(mask, labels):
    return jnp.where(mask[:, None] > 0, labels, jnp.zeros_like(labels))


def after(block, done):
    return lax.optimization_barrier((block, done))[0]


def listed(blocks_ref, counts_ref, tile, groups):
    base = lax.axis_index("shard") * groups
    count = counts_ref[tile]
    ids = [blocks_ref[tile, k] - base for k in range(K)]
    return [
        sum(jnp.where((ids[k] == w) & (k < count), 1, 0) for k in range(K))
        for w in range(groups + SPILL)
    ]


def squares(tiles):
    return functools.reduce(
        jnp.add,
        [
            jnp.square(t[:, h * 128:(h + 1) * 128].astype(jnp.float32))
            for t in tiles
            for h in range(t.shape[1] // 128)
        ],
    )


def row_norms(tiles):
    return jnp.sum(squares(tiles), axis=1, keepdims=True) * SCALE


def column_terms(rows, tiles):
    dots = functools.reduce(
        jnp.add,
        [
            lax.dot_general(r, t, NT, preferred_element_type=jnp.float32)
            for r, t in zip(rows, tiles)
        ],
    )
    return dots * (2.0 * SCALE) - jnp.sum(squares(tiles).T, axis=0, keepdims=True) * SCALE


def early_kernel(
    groups, m, blocks_ref, counts_ref, clusters_ref, own_ref, other_ref, part_ref, factor_ref,
    row_ref,
):
    core = lax.rem(lax.axis_index("grp"), 2)
    eye = lax.broadcasted_iota(jnp.int32, (TILE, TILE), 0) == lax.broadcasted_iota(
        jnp.int32, (TILE, TILE), 1
    )
    tile = 2 * m + core
    at = pl.ds(pl.multiple_of(tile * TILE, TILE), TILE)
    rows = [own_ref[at, :], other_ref[at, :]]
    norms = row_norms(rows)
    own = clusters_ref[:, at].astype(jnp.float32)
    own = jnp.sum(jnp.where(eye, own, jnp.zeros_like(own)), axis=1, keepdims=True)
    row_ref[:, :128] = jnp.broadcast_to(own, (TILE, 128))
    row_ref[:, 128:] = jnp.broadcast_to(norms, (TILE, 128))
    for w, mult in enumerate(listed(blocks_ref, counts_ref, tile, groups)):
        columns = slice(w * TILE, (w + 1) * TILE)
        factor = jnp.full((1, TILE), mult.astype(jnp.float32))
        factor_ref[:, columns] = jnp.broadcast_to(factor, (8, TILE))
        if w < groups:
            cluster = clusters_ref[:, columns].astype(jnp.float32)
            allowed = own == jnp.where(factor > 0, cluster, -1.0)
            if w // 2 == m:
                allowed = allowed & jnp.logical_not(eye & (tile == w))
            terms = column_terms(rows, [own_ref[columns, :], other_ref[columns, :]])
            part_ref[w] = jnp.where(allowed, terms - norms, MASKED)


def rows_of(columns, m, quarters):
    core = lax.rem(lax.axis_index("grp"), 2)
    return [jnp.where(core == 0, columns(2 * m, q), columns(2 * m + 1, q)) for q in quarters]


def logit_kernel(
    groups, m, windows, part_ref, factor_ref, row_ref, own_ref, other_ref, near_ref,
    near_other_ref, *refs,
):
    ins, logit_ref = refs[:-1], refs[-1]
    quarters = range(2, groups)
    core = lax.rem(lax.axis_index("grp"), 2)

    def columns(w, q):
        ref, row = windows[q][w]
        return ins[ref][row:row + TILE, :]

    rows = rows_of(columns, m, quarters)
    norms = row_norms(rows)
    for w in range(groups):
        logit_ref[w] = (
            part_ref[w] - norms + column_terms(rows, [columns(w, q) for q in quarters])
        )
    at = pl.ds(pl.multiple_of((2 * m + core) * TILE, TILE), TILE)
    rows = [own_ref[at, :], other_ref[at, :]]
    norms = norms + row_ref[:, 128:129]
    packed = near_ref[SPILL * TILE:, :].astype(jnp.float32)
    width = packed.shape[1]
    for t in range(SPILL):
        w = groups + t
        cluster = jnp.concatenate(
            [packed[i // width:i // width + 1, :] for i in range(t * TILE, (t + 1) * TILE, width)],
            axis=1,
        )
        factor = factor_ref[0:1, w * TILE:(w + 1) * TILE]
        allowed = row_ref[:, 0:1] == jnp.where(factor > 0, cluster, -1.0)
        tiles = [ref[t * TILE:(t + 1) * TILE, :] for ref in (near_ref, near_other_ref)]
        logit_ref[w] = jnp.where(allowed, column_terms(rows, tiles) - norms, MASKED)


def spread(aff_ref, parts, seed):
    total = jnp.zeros(seed.shape, jnp.float32)
    for w, ref in parts:
        total += jnp.dot(aff_ref[w], ref[...], preferred_element_type=jnp.float32)
    return (spread_weight * total + (1.0 - spread_weight) * seed.astype(jnp.float32)).astype(
        jnp.bfloat16
    )


def affinity_kernel(groups, m, windows, logit_ref, factor_ref, *refs):
    half = groups // 2
    wtiles = groups + SPILL
    ins, (aff_ref, labels_ref, late_ref) = refs[:-3], refs[-3:]
    member = lax.axis_index("grp")
    core = lax.rem(member, 2)
    pair = member // 2
    quarters = range(2, groups)

    def piece(at):
        ref, row = at
        return ins[ref].at[row:row + TILE, :]

    def columns(w, q):
        return piece(windows["x"][q][w])[...]

    rows = rows_of(columns, m, quarters)
    for t in range(SPILL):
        late_ref[t] = logit_ref[groups + t] + column_terms(
            rows, [columns(groups + t, q) for q in quarters]
        )

    def softmax(step, carry):
        at = pl.ds(pl.multiple_of(step * ROWS, ROWS), ROWS)
        logits = [logit_ref[w, at, :] for w in range(groups)]
        logits += [late_ref[t, at, :] for t in range(SPILL)]
        top = jnp.max(functools.reduce(jnp.maximum, logits), axis=1, keepdims=True)
        weights = [
            jnp.exp2(logits[w] - top) * factor_ref[0:1, w * TILE:(w + 1) * TILE]
            for w in range(wtiles)
        ]
        total = jnp.sum(functools.reduce(jnp.add, weights), axis=1, keepdims=True)
        share = 1.0 / total
        for w in range(wtiles):
            aff_ref[w, at, :] = (weights[w] * share).astype(jnp.bfloat16)
        return carry

    lax.fori_loop(0, TILE // ROWS, softmax, 0, unroll=True)

    parts = []
    for r in range(half):
        parts.append((2 * (pair ^ r) + core, piece(windows["mine"][r])))
        parts.append((2 * (pair ^ r) + 1 - core, piece(windows["other"][r])))
    parts.append((groups + core, piece(windows["mine"][half])))
    parts.append((groups + 1 - core, piece(windows["other"][half])))
    seed = piece(windows["mine"][0])[...]
    for r in range(1, half):
        seed = jnp.where((pair ^ m) == r, piece(windows["mine"][r])[...], seed)
    labels_ref[...] = spread(aff_ref, parts, seed)


def own_kernel(groups, seed_ref, *refs):
    half = groups // 2
    core = lax.rem(lax.axis_index("grp"), 2)
    affs, mine, other, out_ref = refs[:half], refs[half:2 * half], refs[2 * half:3 * half], refs[-1]
    for p in range(half):
        @pl.when(lax.axis_index("grp") // 2 == p)
        def _(p=p):
            total = jnp.zeros(out_ref.shape, jnp.float32)
            for m in range(half):
                for w, ref in ((2 * m + core, mine[m]), (2 * m + 1 - core, other[m])):
                    total += jnp.dot(affs[p][w], ref[...], preferred_element_type=jnp.float32)
            out_ref[...] = spread_weight * total + (1.0 - spread_weight) * seed_ref[...].astype(
                jnp.float32
            )


def near_kernel(groups, distance, total_ref, labels_ref, *refs):
    affs, out_ref = refs[:-1], refs[-1]
    core = lax.rem(lax.axis_index("grp"), 2)
    for p in range(groups // 2):
        @pl.when(lax.axis_index("grp") // 2 == p)
        def _(p=p):
            out_ref[...] = (
                total_ref[...]
                + spread_weight
                * jnp.dot(
                    affs[p][groups + (core ^ distance)], labels_ref[...],
                    preferred_element_type=jnp.float32,
                )
            ).astype(out_ref.dtype)


def local(embeddings, clusters, blocks, counts, seed_mask, prior):
    groups = lax.axis_size("grp")
    half = groups // 2
    apart = range(1, half)
    pair = lax.axis_index("grp") // 2
    width = embeddings.shape[1]
    concepts = prior.shape[1]
    wtiles = groups + SPILL
    head_rows = SPILL * TILE
    smem = pl.BlockSpec(memory_space=pltpu.SMEM)
    vmem = pl.BlockSpec(memory_space=pltpu.VMEM)
    params = pltpu.CompilerParams(vmem_limit_bytes=40 * 1024 * 1024)
    little = pl.CostEstimate(flops=1, bytes_accessed=1, transcendentals=0)
    labels_shape = jax.ShapeDtypeStruct((TILE, concepts), jnp.bfloat16)

    first_far = [
        tuple(across(b, 2 * m) for b in tile_and(embeddings[:2 * TILE], prior)) for m in apart
    ]
    mask_far = [across(seed_mask, 2 * m) for m in apart]
    rest_far = [across(embeddings[TILE:], 2 * m) for m in apart]

    head_c = clusters[:head_rows].astype(jnp.bfloat16).reshape(-1, width)
    head_c = jnp.pad(head_c, ((0, 16 - head_c.shape[0]), (0, 0)))
    head = jnp.concatenate([embeddings[:head_rows], head_c])
    near = from_next(head)

    own_other = across(after(embeddings, head), 1)
    near_other = across(near, 1)

    def early_of(m, done=()):
        own, other = after((embeddings, own_other), done) if m else (embeddings, own_other)
        return pl.pallas_call(
            functools.partial(early_kernel, groups, m),
            out_shape=(
                jax.ShapeDtypeStruct((groups, TILE, TILE), jnp.float32),
                jax.ShapeDtypeStruct((8, wtiles * TILE), jnp.float32),
                jax.ShapeDtypeStruct((TILE, 256), jnp.float32),
            ),
            in_specs=[smem, smem] + [vmem] * 3,
            out_specs=(vmem, vmem, vmem),
            compiler_params=params,
            cost_estimate=little,
            name=f"early_{m}",
        )(blocks, counts, clusters.reshape(1, -1), own, other)

    first_early = early_of(0)

    seeds = masked(seed_mask, prior)
    seeds_far = [masked(k, tile_in(f, 1)) for k, f in zip(mask_far, first_far)]
    seeds_far = after(seeds_far, first_early)
    head_seeds = seeds
    for m in apart:
        head_seeds = jnp.where(pair == m, seeds_far[m - 1], head_seeds)
    first_on = [bundle(tile_in(first_far[0], 0), head_seeds)]
    first_on += [(tile_in(f, 0),) for f in first_far[1:]]
    near_first = [tuple(from_next(b) for b in f) for f in first_on]

    near_second = [across(near[TILE:head_rows], 2 * m) for m in apart]

    first_far_other = [across(tile_in(f, 0), 1) for f in first_far]
    rest_far_other = [(across(f[:TILE], 1), across(f[TILE:], 1)) for f in rest_far]
    seeds_other = across(after(seeds, first_far_other), 1)
    seeds_far_other = [across(f, 1) for f in seeds_far]

    own_arrays = []
    own_windows = [None, None]
    for m in range(half - 1):
        at = len(own_arrays)
        own_arrays += [first_far[m][0], rest_far[m], first_far_other[m], *rest_far_other[m]]
        own_windows.append([(at, 0)] + [(at + 1, t * TILE) for t in range(groups - 1)])
        own_windows.append([(at + 2, 0), (at + 3, 0)] + [(at + 4, t * TILE) for t in range(groups - 2)])

    def logits_of(m, early):
        return pl.pallas_call(
            functools.partial(logit_kernel, groups, m, own_windows),
            out_shape=jax.ShapeDtypeStruct((wtiles, TILE, TILE), jnp.float32),
            in_specs=[vmem] * (7 + len(own_arrays)),
            out_specs=vmem,
            compiler_params=params,
            cost_estimate=little,
            name=f"logits_{m}",
        )(*early, embeddings, own_other, near, near_other, *own_arrays)

    first_logits = logits_of(0, first_early)
    near_second_other = [across(f, 1) for f in near_second]
    near_first_other = [tuple(across(b, 1) for b in f) for f in near_first]

    arrays = []

    def place(*blocks):
        out = []
        for block, tiles in blocks:
            at = [i for i, a in enumerate(arrays) if a is block]
            if not at:
                arrays.append(block)
                at = [len(arrays) - 1]
            out += [(at[0], t * TILE) for t in tiles]
        return out

    def seeds_in(f):
        return (f[0], [1]) if len(f) == 1 else (f[1], [0])

    windows = {"x": [None, None], "mine": place((seeds, [0])), "other": place((seeds_other, [0]))}
    for m in range(half - 1):
        windows["x"].append(
            place(
                (first_far[m][0], [0]), (rest_far[m], range(groups - 1)),
                (near_first[m][0], [0]), (near_second[m], [0]),
            )
        )
        one, more = rest_far_other[m]
        windows["x"].append(
            place(
                (first_far_other[m], [0]), (one, [0]), (more, range(groups - 2)),
                (near_first_other[m][0], [0]), (near_second_other[m], [0]),
            )
        )
        windows["mine"] += place((seeds_far[m], [0]))
        windows["other"] += place((seeds_far_other[m], [0]))
    windows["mine"] += place(seeds_in(near_first[0]))
    windows["other"] += place(seeds_in(near_first_other[0]))

    def affinity_of(m, done):
        early = early_of(m, done) if m else first_early
        logits = logits_of(m, early) if m else first_logits
        return pl.pallas_call(
            functools.partial(affinity_kernel, groups, m, windows),
            out_shape=(jax.ShapeDtypeStruct((wtiles, TILE, TILE), jnp.bfloat16), labels_shape),
            in_specs=[vmem] * (2 + len(arrays)),
            out_specs=(vmem, vmem),
            scratch_shapes=[pltpu.VMEM((SPILL, TILE, TILE), jnp.float32)],
            compiler_params=params,
            cost_estimate=little,
            name=f"affinity_{m}",
        )(logits, early[1], *arrays)

    affinity, labels = [], []
    for m in range(half):
        a, l = affinity_of(m, labels[-1:])
        affinity.append(a)
        labels.append(l)
    near_labels = from_next(labels[0])
    near_labels_other = across(near_labels, 1)
    others = [across(l, 1) for l in labels]
    total = pl.pallas_call(
        functools.partial(own_kernel, groups),
        out_shape=jax.ShapeDtypeStruct((TILE, concepts), jnp.float32),
        in_specs=[vmem] * (1 + 3 * half),
        out_specs=vmem,
        compiler_params=params,
        cost_estimate=little,
        name="spread_own",
    )(seeds, *affinity, *labels, *others)
    for distance, block in enumerate((near_labels, near_labels_other)):
        total = pl.pallas_call(
            functools.partial(near_kernel, groups, distance),
            out_shape=jax.ShapeDtypeStruct((TILE, concepts), jnp.bfloat16 if distance else jnp.float32),
            in_specs=[vmem] * (2 + half),
            out_specs=vmem,
            compiler_params=params,
            cost_estimate=little,
            name=f"spread_near_{distance}",
        )(total, block, *affinity)
    return total


def solution(mesh):
    in_specs = (
        P("shard", "grp"),
        P("shard"),
        P("shard", None),
        P("shard"),
        P(("shard", "grp")),
        P(("shard", "grp"), None),
    )
    out_specs = P(("shard", "grp"), None)
    return jax.shard_map(local, mesh=mesh, in_specs=in_specs, out_specs=out_specs, check_vma=False)
```

```python
import functools

import jax
import jax.numpy as jnp
from jax import lax
from jax.experimental import pallas as pl
from jax.experimental.pallas import tpu as pltpu
from jax.sharding import PartitionSpec as P

TILE = 256
K = 4
SPILL = 2
ROWS = 32

kernel_width = 0.06
spread_weight = 0.6
MASKED = -1e30
SCALE = 1.4426950408889634 / kernel_width

NT = (((1,), (1,)), ((), ()))


def across(block, distance):
    groups = lax.axis_size("grp")
    return lax.ppermute(block, "grp", [(i, i ^ distance) for i in range(groups)])


def from_next(block):
    shards = lax.axis_size("shard")
    return lax.ppermute(block, "shard", [(i + 1, i) for i in range(shards - 1)])


def bundle(*blocks):
    if len({b.shape[1] for b in blocks}) == 1:
        return (jnp.concatenate(blocks),)
    return blocks


def tile_and(tiles, block):
    if tiles.shape[1] != block.shape[1]:
        return tiles[:TILE], block
    first = lax.broadcasted_iota(jnp.int32, tiles.shape, 0) < TILE
    return (jnp.where(first, tiles, jnp.concatenate([block, block])),)


def tile_in(blocks, t):
    return blocks[0][t * TILE:(t + 1) * TILE] if len(blocks) == 1 else blocks[t]


def masked(mask, labels):
    return jnp.where(mask[:, None] > 0, labels, jnp.zeros_like(labels))


def after(block, done):
    return lax.optimization_barrier((block, done))[0]


def listed(blocks_ref, counts_ref, tile, groups):
    base = lax.axis_index("shard") * groups
    count = counts_ref[tile]
    ids = [blocks_ref[tile, k] - base for k in range(K)]
    return [
        sum(jnp.where((ids[k] == w) & (k < count), 1, 0) for k in range(K))
        for w in range(groups + SPILL)
    ]


def squares(tiles):
    return functools.reduce(
        jnp.add,
        [
            jnp.square(t[:, h * 128:(h + 1) * 128].astype(jnp.float32))
            for t in tiles
            for h in range(t.shape[1] // 128)
        ],
    )


def row_norms(tiles):
    return jnp.sum(squares(tiles), axis=1, keepdims=True) * SCALE


def column_terms(rows, tiles):
    dots = functools.reduce(
        jnp.add,
        [
            lax.dot_general(r, t, NT, preferred_element_type=jnp.float32)
            for r, t in zip(rows, tiles)
        ],
    )
    return dots * (2.0 * SCALE) - jnp.sum(squares(tiles).T, axis=0, keepdims=True) * SCALE


def early_kernel(
    groups, m, blocks_ref, counts_ref, clusters_ref, own_ref, other_ref, part_ref, factor_ref,
    row_ref,
):
    core = lax.rem(lax.axis_index("grp"), 2)
    eye = lax.broadcasted_iota(jnp.int32, (TILE, TILE), 0) == lax.broadcasted_iota(
        jnp.int32, (TILE, TILE), 1
    )
    tile = 2 * m + core
    at = pl.ds(pl.multiple_of(tile * TILE, TILE), TILE)
    rows = [own_ref[at, :], other_ref[at, :]]
    norms = row_norms(rows)
    own = clusters_ref[:, at].astype(jnp.float32)
    own = jnp.sum(jnp.where(eye, own, jnp.zeros_like(own)), axis=1, keepdims=True)
    row_ref[:, :128] = jnp.broadcast_to(own, (TILE, 128))
    row_ref[:, 128:] = jnp.broadcast_to(norms, (TILE, 128))
    for w, mult in enumerate(listed(blocks_ref, counts_ref, tile, groups)):
        columns = slice(w * TILE, (w + 1) * TILE)
        factor = jnp.full((1, TILE), mult.astype(jnp.float32))
        factor_ref[:, columns] = jnp.broadcast_to(factor, (8, TILE))
        if w < groups:
            cluster = clusters_ref[:, columns].astype(jnp.float32)
            allowed = own == jnp.where(factor > 0, cluster, -1.0)
            if w // 2 == m:
                allowed = allowed & jnp.logical_not(eye & (tile == w))
            terms = column_terms(rows, [own_ref[columns, :], other_ref[columns, :]])
            part_ref[w] = jnp.where(allowed, terms - norms, MASKED)


def rows_of(columns, m, quarters):
    core = lax.rem(lax.axis_index("grp"), 2)
    return [jnp.where(core == 0, columns(2 * m, q), columns(2 * m + 1, q)) for q in quarters]


def logit_kernel(
    groups, m, windows, part_ref, factor_ref, row_ref, own_ref, other_ref, near_ref,
    near_other_ref, *refs,
):
    ins, logit_ref = refs[:-1], refs[-1]
    quarters = range(2, groups)
    core = lax.rem(lax.axis_index("grp"), 2)

    def columns(w, q):
        ref, row = windows[q][w]
        return ins[ref][row:row + TILE, :]

    rows = rows_of(columns, m, quarters)
    norms = row_norms(rows)
    for w in range(groups):
        logit_ref[w] = (
            part_ref[w] - norms + column_terms(rows, [columns(w, q) for q in quarters])
        )
    at = pl.ds(pl.multiple_of((2 * m + core) * TILE, TILE), TILE)
    rows = [own_ref[at, :], other_ref[at, :]]
    norms = norms + row_ref[:, 128:129]
    packed = near_ref[SPILL * TILE:, :].astype(jnp.float32)
    width = packed.shape[1]
    for t in range(SPILL):
        w = groups + t
        cluster = jnp.concatenate(
            [packed[i // width:i // width + 1, :] for i in range(t * TILE, (t + 1) * TILE, width)],
            axis=1,
        )
        factor = factor_ref[0:1, w * TILE:(w + 1) * TILE]
        allowed = row_ref[:, 0:1] == jnp.where(factor > 0, cluster, -1.0)
        tiles = [ref[t * TILE:(t + 1) * TILE, :] for ref in (near_ref, near_other_ref)]
        logit_ref[w] = jnp.where(allowed, column_terms(rows, tiles) - norms, MASKED)


def spread(aff_ref, parts, seed):
    total = jnp.zeros(seed.shape, jnp.float32)
    for w, ref in parts:
        total += jnp.dot(aff_ref[w], ref[...], preferred_element_type=jnp.float32)
    return (spread_weight * total + (1.0 - spread_weight) * seed.astype(jnp.float32)).astype(
        jnp.bfloat16
    )


def affinity_kernel(groups, m, windows, logit_ref, factor_ref, *refs):
    half = groups // 2
    wtiles = groups + SPILL
    ins, (aff_ref, labels_ref, late_ref) = refs[:-3], refs[-3:]
    member = lax.axis_index("grp")
    core = lax.rem(member, 2)
    pair = member // 2
    quarters = range(2, groups)

    def piece(at):
        ref, row = at
        return ins[ref].at[row:row + TILE, :]

    def columns(w, q):
        return piece(windows["x"][q][w])[...]

    rows = rows_of(columns, m, quarters)
    for t in range(SPILL):
        late_ref[t] = logit_ref[groups + t] + column_terms(
            rows, [columns(groups + t, q) for q in quarters]
        )

    def softmax(step, carry):
        at = pl.ds(pl.multiple_of(step * ROWS, ROWS), ROWS)
        logits = [logit_ref[w, at, :] for w in range(groups)]
        logits += [late_ref[t, at, :] for t in range(SPILL)]
        top = jnp.max(functools.reduce(jnp.maximum, logits), axis=1, keepdims=True)
        weights = [
            jnp.exp2(logits[w] - top) * factor_ref[0:1, w * TILE:(w + 1) * TILE]
            for w in range(wtiles)
        ]
        total = jnp.sum(functools.reduce(jnp.add, weights), axis=1, keepdims=True)
        share = 1.0 / total
        for w in range(wtiles):
            aff_ref[w, at, :] = (weights[w] * share).astype(jnp.bfloat16)
        return carry

    lax.fori_loop(0, TILE // ROWS, softmax, 0, unroll=True)

    parts = []
    for r in range(half):
        parts.append((2 * (pair ^ r) + core, piece(windows["mine"][r])))
        parts.append((2 * (pair ^ r) + 1 - core, piece(windows["other"][r])))
    parts.append((groups + core, piece(windows["mine"][half])))
    parts.append((groups + 1 - core, piece(windows["other"][half])))
    seed = piece(windows["mine"][0])[...]
    for r in range(1, half):
        seed = jnp.where((pair ^ m) == r, piece(windows["mine"][r])[...], seed)
    labels_ref[...] = spread(aff_ref, parts, seed)


def own_kernel(groups, seed_ref, *refs):
    half = groups // 2
    core = lax.rem(lax.axis_index("grp"), 2)
    affs, mine, other, out_ref = refs[:half], refs[half:2 * half], refs[2 * half:3 * half], refs[-1]
    for p in range(half):
        @pl.when(lax.axis_index("grp") // 2 == p)
        def _(p=p):
            total = jnp.zeros(out_ref.shape, jnp.float32)
            for m in range(half):
                for w, ref in ((2 * m + core, mine[m]), (2 * m + 1 - core, other[m])):
                    total += jnp.dot(affs[p][w], ref[...], preferred_element_type=jnp.float32)
            out_ref[...] = spread_weight * total + (1.0 - spread_weight) * seed_ref[...].astype(
                jnp.float32
            )


def near_kernel(groups, distance, total_ref, labels_ref, *refs):
    affs, out_ref = refs[:-1], refs[-1]
    core = lax.rem(lax.axis_index("grp"), 2)
    for p in range(groups // 2):
        @pl.when(lax.axis_index("grp") // 2 == p)
        def _(p=p):
            out_ref[...] = (
                total_ref[...]
                + spread_weight
                * jnp.dot(
                    affs[p][groups + (core ^ distance)], labels_ref[...],
                    preferred_element_type=jnp.float32,
                )
            ).astype(out_ref.dtype)


def local(embeddings, clusters, blocks, counts, seed_mask, prior):
    groups = lax.axis_size("grp")
    half = groups // 2
    apart = range(1, half)
    pair = lax.axis_index("grp") // 2
    width = embeddings.shape[1]
    concepts = prior.shape[1]
    wtiles = groups + SPILL
    head_rows = SPILL * TILE
    smem = pl.BlockSpec(memory_space=pltpu.SMEM)
    vmem = pl.BlockSpec(memory_space=pltpu.VMEM)
    params = pltpu.CompilerParams(vmem_limit_bytes=40 * 1024 * 1024)
    little = pl.CostEstimate(flops=1, bytes_accessed=1, transcendentals=0)
    labels_shape = jax.ShapeDtypeStruct((TILE, concepts), jnp.bfloat16)

    first_far = [
        tuple(across(b, 2 * m) for b in tile_and(embeddings[:2 * TILE], prior)) for m in apart
    ]
    mask_far = [across(seed_mask, 2 * m) for m in apart]
    rest_far = [across(embeddings[TILE:], 2 * m) for m in apart]

    head_c = clusters[:head_rows].astype(jnp.bfloat16).reshape(-1, width)
    head_c = jnp.pad(head_c, ((0, 16 - head_c.shape[0]), (0, 0)))
    head = jnp.concatenate([embeddings[:head_rows], head_c])
    near = from_next(head)

    own_other = across(after(embeddings, head), 1)
    near_other = across(near, 1)

    def early_of(m, done=()):
        own, other = after((embeddings, own_other), done) if m else (embeddings, own_other)
        return pl.pallas_call(
            functools.partial(early_kernel, groups, m),
            out_shape=(
                jax.ShapeDtypeStruct((groups, TILE, TILE), jnp.float32),
                jax.ShapeDtypeStruct((8, wtiles * TILE), jnp.float32),
                jax.ShapeDtypeStruct((TILE, 256), jnp.float32),
            ),
            in_specs=[smem, smem] + [vmem] * 3,
            out_specs=(vmem, vmem, vmem),
            compiler_params=params,
            cost_estimate=little,
            name=f"early_{m}",
        )(blocks, counts, clusters.reshape(1, -1), own, other)

    first_early = early_of(0)

    seeds = masked(seed_mask, prior)
    seeds_far = [masked(k, tile_in(f, 1)) for k, f in zip(mask_far, first_far)]
    seeds_far = after(seeds_far, first_early)
    head_seeds = seeds
    for m in apart:
        head_seeds = jnp.where(pair == m, seeds_far[m - 1], head_seeds)
    first_on = [bundle(tile_in(first_far[0], 0), head_seeds)]
    first_on += [(tile_in(f, 0),) for f in first_far[1:]]
    near_first = [tuple(from_next(b) for b in f) for f in first_on]

    near_second = [across(near[TILE:head_rows], 2 * m) for m in apart]

    first_far_other = [across(tile_in(f, 0), 1) for f in first_far]
    rest_far_other = [(across(f[:TILE], 1), across(f[TILE:], 1)) for f in rest_far]
    seeds_other = across(seeds, 1)
    seeds_far_other = [across(f, 1) for f in seeds_far]

    own_arrays = []
    own_windows = [None, None]
    for m in range(half - 1):
        at = len(own_arrays)
        own_arrays += [first_far[m][0], rest_far[m], first_far_other[m], *rest_far_other[m]]
        own_windows.append([(at, 0)] + [(at + 1, t * TILE) for t in range(groups - 1)])
        own_windows.append([(at + 2, 0), (at + 3, 0)] + [(at + 4, t * TILE) for t in range(groups - 2)])

    def logits_of(m, early):
        return pl.pallas_call(
            functools.partial(logit_kernel, groups, m, own_windows),
            out_shape=jax.ShapeDtypeStruct((wtiles, TILE, TILE), jnp.float32),
            in_specs=[vmem] * (7 + len(own_arrays)),
            out_specs=vmem,
            compiler_params=params,
            cost_estimate=little,
            name=f"logits_{m}",
        )(*early, embeddings, own_other, near, near_other, *own_arrays)

    first_logits = logits_of(0, first_early)
    near_second_other = [across(f, 1) for f in near_second]
    near_first_other = [tuple(across(b, 1) for b in f) for f in near_first]

    arrays = []

    def place(*blocks):
        out = []
        for block, tiles in blocks:
            at = [i for i, a in enumerate(arrays) if a is block]
            if not at:
                arrays.append(block)
                at = [len(arrays) - 1]
            out += [(at[0], t * TILE) for t in tiles]
        return out

    def seeds_in(f):
        return (f[0], [1]) if len(f) == 1 else (f[1], [0])

    windows = {"x": [None, None], "mine": place((seeds, [0])), "other": place((seeds_other, [0]))}
    for m in range(half - 1):
        windows["x"].append(
            place(
                (first_far[m][0], [0]), (rest_far[m], range(groups - 1)),
                (near_first[m][0], [0]), (near_second[m], [0]),
            )
        )
        one, more = rest_far_other[m]
        windows["x"].append(
            place(
                (first_far_other[m], [0]), (one, [0]), (more, range(groups - 2)),
                (near_first_other[m][0], [0]), (near_second_other[m], [0]),
            )
        )
        windows["mine"] += place((seeds_far[m], [0]))
        windows["other"] += place((seeds_far_other[m], [0]))
    windows["mine"] += place(seeds_in(near_first[0]))
    windows["other"] += place(seeds_in(near_first_other[0]))

    def affinity_of(m, done):
        early = early_of(m, done) if m else first_early
        logits = logits_of(m, early) if m else first_logits
        return pl.pallas_call(
            functools.partial(affinity_kernel, groups, m, windows),
            out_shape=(jax.ShapeDtypeStruct((wtiles, TILE, TILE), jnp.bfloat16), labels_shape),
            in_specs=[vmem] * (2 + len(arrays)),
            out_specs=(vmem, vmem),
            scratch_shapes=[pltpu.VMEM((SPILL, TILE, TILE), jnp.float32)],
            compiler_params=params,
            cost_estimate=little,
            name=f"affinity_{m}",
        )(logits, early[1], *arrays)

    affinity, labels = [], []
    for m in range(half):
        a, l = affinity_of(m, labels[-1:])
        affinity.append(a)
        labels.append(l)
    near_labels = from_next(labels[0])
    near_labels_other = across(near_labels, 1)
    others = [across(l, 1) for l in labels]
    total = pl.pallas_call(
        functools.partial(own_kernel, groups),
        out_shape=jax.ShapeDtypeStruct((TILE, concepts), jnp.float32),
        in_specs=[vmem] * (1 + 3 * half),
        out_specs=vmem,
        compiler_params=params,
        cost_estimate=little,
        name="spread_own",
    )(seeds, *affinity, *labels, *others)
    for distance, block in enumerate((near_labels, near_labels_other)):
        total = pl.pallas_call(
            functools.partial(near_kernel, groups, distance),
            out_shape=jax.ShapeDtypeStruct((TILE, concepts), jnp.bfloat16 if distance else jnp.float32),
            in_specs=[vmem] * (2 + half),
            out_specs=vmem,
            compiler_params=params,
            cost_estimate=little,
            name=f"spread_near_{distance}",
        )(total, block, *affinity)
    return total


def solution(mesh):
    in_specs = (
        P("shard", "grp"),
        P("shard"),
        P("shard", None),
        P("shard"),
        P(("shard", "grp")),
        P(("shard", "grp"), None),
    )
    out_specs = P(("shard", "grp"), None)
    return jax.shard_map(local, mesh=mesh, in_specs=in_specs, out_specs=out_specs, check_vma=False)
```

```python
import functools

import jax
import jax.numpy as jnp
from jax import lax
from jax.experimental import pallas as pl
from jax.experimental.pallas import tpu as pltpu
from jax.sharding import PartitionSpec as P

TILE = 256
K = 4
SPILL = 2
ROWS = 32

kernel_width = 0.06
spread_weight = 0.6
MASKED = -1e30
SCALE = 1.4426950408889634 / kernel_width

NT = (((1,), (1,)), ((), ()))


def across(block, distance):
    groups = lax.axis_size("grp")
    return lax.ppermute(block, "grp", [(i, i ^ distance) for i in range(groups)])


def from_next(block):
    shards = lax.axis_size("shard")
    return lax.ppermute(block, "shard", [(i + 1, i) for i in range(shards - 1)])


def bundle(*blocks):
    if len({b.shape[1] for b in blocks}) == 1:
        return (jnp.concatenate(blocks),)
    return blocks


def tile_and(tiles, block):
    if tiles.shape[1] != block.shape[1]:
        return tiles[:TILE], block
    first = lax.broadcasted_iota(jnp.int32, tiles.shape, 0) < TILE
    return (jnp.where(first, tiles, jnp.concatenate([block, block])),)


def tile_in(blocks, t):
    return blocks[0][t * TILE:(t + 1) * TILE] if len(blocks) == 1 else blocks[t]


def masked(mask, labels):
    return jnp.where(mask[:, None] > 0, labels, jnp.zeros_like(labels))


def after(block, done):
    return lax.optimization_barrier((block, done))[0]


def listed(blocks_ref, counts_ref, tile, groups):
    base = lax.axis_index("shard") * groups
    count = counts_ref[tile]
    ids = [blocks_ref[tile, k] - base for k in range(K)]
    return [
        sum(jnp.where((ids[k] == w) & (k < count), 1, 0) for k in range(K))
        for w in range(groups + SPILL)
    ]


def squares(tiles):
    return functools.reduce(
        jnp.add,
        [
            jnp.square(t[:, h * 128:(h + 1) * 128].astype(jnp.float32))
            for t in tiles
            for h in range(t.shape[1] // 128)
        ],
    )


def row_norms(tiles):
    return jnp.sum(squares(tiles), axis=1, keepdims=True) * SCALE


def column_terms(rows, tiles):
    dots = functools.reduce(
        jnp.add,
        [
            lax.dot_general(r, t, NT, preferred_element_type=jnp.float32)
            for r, t in zip(rows, tiles)
        ],
    )
    return dots * (2.0 * SCALE) - jnp.sum(squares(tiles).T, axis=0, keepdims=True) * SCALE


def early_kernel(
    groups, m, blocks_ref, counts_ref, clusters_ref, own_ref, other_ref, part_ref, factor_ref,
    row_ref,
):
    core = lax.rem(lax.axis_index("grp"), 2)
    eye = lax.broadcasted_iota(jnp.int32, (TILE, TILE), 0) == lax.broadcasted_iota(
        jnp.int32, (TILE, TILE), 1
    )
    tile = 2 * m + core
    at = pl.ds(pl.multiple_of(tile * TILE, TILE), TILE)
    rows = [own_ref[at, :], other_ref[at, :]]
    norms = row_norms(rows)
    own = clusters_ref[:, at].astype(jnp.float32)
    own = jnp.sum(jnp.where(eye, own, jnp.zeros_like(own)), axis=1, keepdims=True)
    row_ref[:, :128] = jnp.broadcast_to(own, (TILE, 128))
    row_ref[:, 128:] = jnp.broadcast_to(norms, (TILE, 128))
    for w, mult in enumerate(listed(blocks_ref, counts_ref, tile, groups)):
        columns = slice(w * TILE, (w + 1) * TILE)
        factor = jnp.full((1, TILE), mult.astype(jnp.float32))
        factor_ref[:, columns] = jnp.broadcast_to(factor, (8, TILE))
        if w < groups:
            cluster = clusters_ref[:, columns].astype(jnp.float32)
            allowed = own == jnp.where(factor > 0, cluster, -1.0)
            if w // 2 == m:
                allowed = allowed & jnp.logical_not(eye & (tile == w))
            terms = column_terms(rows, [own_ref[columns, :], other_ref[columns, :]])
            part_ref[w] = jnp.where(allowed, terms - norms, MASKED)


def rows_of(columns, m, quarters):
    core = lax.rem(lax.axis_index("grp"), 2)
    return [jnp.where(core == 0, columns(2 * m, q), columns(2 * m + 1, q)) for q in quarters]


def logit_kernel(
    groups, m, windows, part_ref, factor_ref, row_ref, own_ref, other_ref, near_ref,
    near_other_ref, *refs,
):
    ins, logit_ref = refs[:-1], refs[-1]
    quarters = range(2, groups)
    core = lax.rem(lax.axis_index("grp"), 2)

    def columns(w, q):
        ref, row = windows[q][w]
        return ins[ref][row:row + TILE, :]

    rows = rows_of(columns, m, quarters)
    norms = row_norms(rows)
    for w in range(groups):
        logit_ref[w] = (
            part_ref[w] - norms + column_terms(rows, [columns(w, q) for q in quarters])
        )
    at = pl.ds(pl.multiple_of((2 * m + core) * TILE, TILE), TILE)
    rows = [own_ref[at, :], other_ref[at, :]]
    norms = norms + row_ref[:, 128:129]
    packed = near_ref[SPILL * TILE:, :].astype(jnp.float32)
    width = packed.shape[1]
    for t in range(SPILL):
        w = groups + t
        cluster = jnp.concatenate(
            [packed[i // width:i // width + 1, :] for i in range(t * TILE, (t + 1) * TILE, width)],
            axis=1,
        )
        factor = factor_ref[0:1, w * TILE:(w + 1) * TILE]
        allowed = row_ref[:, 0:1] == jnp.where(factor > 0, cluster, -1.0)
        tiles = [ref[t * TILE:(t + 1) * TILE, :] for ref in (near_ref, near_other_ref)]
        logit_ref[w] = jnp.where(allowed, column_terms(rows, tiles) - norms, MASKED)


def spread(aff_ref, parts, seed):
    total = jnp.zeros(seed.shape, jnp.float32)
    for w, ref in parts:
        total += jnp.dot(aff_ref[w], ref[...], preferred_element_type=jnp.float32)
    return (spread_weight * total + (1.0 - spread_weight) * seed.astype(jnp.float32)).astype(
        jnp.bfloat16
    )


def affinity_kernel(groups, m, windows, logit_ref, factor_ref, *refs):
    half = groups // 2
    wtiles = groups + SPILL
    ins, (aff_ref, labels_ref, late_ref) = refs[:-3], refs[-3:]
    member = lax.axis_index("grp")
    core = lax.rem(member, 2)
    pair = member // 2
    quarters = range(2, groups)

    def piece(at):
        ref, row = at
        return ins[ref].at[row:row + TILE, :]

    def columns(w, q):
        return piece(windows["x"][q][w])[...]

    rows = rows_of(columns, m, quarters)
    for t in range(SPILL):
        late_ref[t] = logit_ref[groups + t] + column_terms(
            rows, [columns(groups + t, q) for q in quarters]
        )

    def softmax(step, carry):
        at = pl.ds(pl.multiple_of(step * ROWS, ROWS), ROWS)
        logits = [logit_ref[w, at, :] for w in range(groups)]
        logits += [late_ref[t, at, :] for t in range(SPILL)]
        top = jnp.max(functools.reduce(jnp.maximum, logits), axis=1, keepdims=True)
        weights = [
            jnp.exp2(logits[w] - top) * factor_ref[0:1, w * TILE:(w + 1) * TILE]
            for w in range(wtiles)
        ]
        total = jnp.sum(functools.reduce(jnp.add, weights), axis=1, keepdims=True)
        share = 1.0 / total
        for w in range(wtiles):
            aff_ref[w, at, :] = (weights[w] * share).astype(jnp.bfloat16)
        return carry

    lax.fori_loop(0, TILE // ROWS, softmax, 0, unroll=True)

    parts = []
    for r in range(half):
        parts.append((2 * (pair ^ r) + core, piece(windows["mine"][r])))
        parts.append((2 * (pair ^ r) + 1 - core, piece(windows["other"][r])))
    parts.append((groups + core, piece(windows["mine"][half])))
    parts.append((groups + 1 - core, piece(windows["other"][half])))
    seed = piece(windows["mine"][0])[...]
    for r in range(1, half):
        seed = jnp.where((pair ^ m) == r, piece(windows["mine"][r])[...], seed)
    labels_ref[...] = spread(aff_ref, parts, seed)


def own_kernel(groups, seed_ref, *refs):
    half = groups // 2
    core = lax.rem(lax.axis_index("grp"), 2)
    affs, mine, other, out_ref = refs[:half], refs[half:2 * half], refs[2 * half:3 * half], refs[-1]
    for p in range(half):
        @pl.when(lax.axis_index("grp") // 2 == p)
        def _(p=p):
            total = jnp.zeros(out_ref.shape, jnp.float32)
            for m in range(half):
                for w, ref in ((2 * m + core, mine[m]), (2 * m + 1 - core, other[m])):
                    total += jnp.dot(affs[p][w], ref[...], preferred_element_type=jnp.float32)
            out_ref[...] = spread_weight * total + (1.0 - spread_weight) * seed_ref[...].astype(
                jnp.float32
            )


def near_kernel(groups, distance, total_ref, labels_ref, *refs):
    affs, out_ref = refs[:-1], refs[-1]
    core = lax.rem(lax.axis_index("grp"), 2)
    for p in range(groups // 2):
        @pl.when(lax.axis_index("grp") // 2 == p)
        def _(p=p):
            out_ref[...] = (
                total_ref[...]
                + spread_weight
                * jnp.dot(
                    affs[p][groups + (core ^ distance)], labels_ref[...],
                    preferred_element_type=jnp.float32,
                )
            ).astype(out_ref.dtype)


def local(embeddings, clusters, blocks, counts, seed_mask, prior):
    groups = lax.axis_size("grp")
    half = groups // 2
    apart = range(1, half)
    pair = lax.axis_index("grp") // 2
    width = embeddings.shape[1]
    concepts = prior.shape[1]
    wtiles = groups + SPILL
    head_rows = SPILL * TILE
    smem = pl.BlockSpec(memory_space=pltpu.SMEM)
    vmem = pl.BlockSpec(memory_space=pltpu.VMEM)
    params = pltpu.CompilerParams(vmem_limit_bytes=40 * 1024 * 1024)
    little = pl.CostEstimate(flops=1, bytes_accessed=1, transcendentals=0)
    labels_shape = jax.ShapeDtypeStruct((TILE, concepts), jnp.bfloat16)

    first_far = [
        tuple(across(b, 2 * m) for b in tile_and(embeddings[:2 * TILE], prior)) for m in apart
    ]
    mask_far = [across(seed_mask, 2 * m) for m in apart]
    rest_far = [across(embeddings[TILE:], 2 * m) for m in apart]

    head_c = clusters[:head_rows].astype(jnp.bfloat16).reshape(-1, width)
    head_c = jnp.pad(head_c, ((0, 16 - head_c.shape[0]), (0, 0)))
    head = jnp.concatenate([embeddings[:head_rows], head_c])
    near = from_next(head)

    own_other = across(after(embeddings, head), 1)
    near_other = across(near, 1)

    def early_of(m, done=()):
        own, other = after((embeddings, own_other), done) if m else (embeddings, own_other)
        return pl.pallas_call(
            functools.partial(early_kernel, groups, m),
            out_shape=(
                jax.ShapeDtypeStruct((groups, TILE, TILE), jnp.float32),
                jax.ShapeDtypeStruct((8, wtiles * TILE), jnp.float32),
                jax.ShapeDtypeStruct((TILE, 256), jnp.float32),
            ),
            in_specs=[smem, smem] + [vmem] * 3,
            out_specs=(vmem, vmem, vmem),
            compiler_params=params,
            cost_estimate=little,
            name=f"early_{m}",
        )(blocks, counts, clusters.reshape(1, -1), own, other)

    first_early = early_of(0)

    seeds = masked(seed_mask, prior)
    seeds_far = [masked(k, tile_in(f, 1)) for k, f in zip(mask_far, first_far)]
    seeds_far = after(seeds_far, first_early)
    head_seeds = seeds
    for m in apart:
        head_seeds = jnp.where(pair == m, seeds_far[m - 1], head_seeds)
    first_on = [bundle(tile_in(first_far[0], 0), head_seeds)]
    first_on += [(tile_in(f, 0),) for f in first_far[1:]]
    near_first = [tuple(from_next(b) for b in f) for f in first_on]

    near_second = [across(near[TILE:head_rows], 2 * m) for m in apart]

    first_far_other = [across(tile_in(f, 0), 1) for f in first_far]
    rest_far_other = [
        (across(f[:TILE], 1), across(after(f[TILE:], first_far_other), 1)) for f in rest_far
    ]
    seeds_other = across(seeds, 1)
    seeds_far_other = [across(f, 1) for f in seeds_far]

    own_arrays = []
    own_windows = [None, None]
    for m in range(half - 1):
        at = len(own_arrays)
        own_arrays += [first_far[m][0], rest_far[m], first_far_other[m], *rest_far_other[m]]
        own_windows.append([(at, 0)] + [(at + 1, t * TILE) for t in range(groups - 1)])
        own_windows.append([(at + 2, 0), (at + 3, 0)] + [(at + 4, t * TILE) for t in range(groups - 2)])

    def logits_of(m, early):
        return pl.pallas_call(
            functools.partial(logit_kernel, groups, m, own_windows),
            out_shape=jax.ShapeDtypeStruct((wtiles, TILE, TILE), jnp.float32),
            in_specs=[vmem] * (7 + len(own_arrays)),
            out_specs=vmem,
            compiler_params=params,
            cost_estimate=little,
            name=f"logits_{m}",
        )(*early, embeddings, own_other, near, near_other, *own_arrays)

    first_logits = logits_of(0, first_early)
    near_second_other = [across(f, 1) for f in near_second]
    near_first_other = [tuple(across(b, 1) for b in f) for f in near_first]

    arrays = []

    def place(*blocks):
        out = []
        for block, tiles in blocks:
            at = [i for i, a in enumerate(arrays) if a is block]
            if not at:
                arrays.append(block)
                at = [len(arrays) - 1]
            out += [(at[0], t * TILE) for t in tiles]
        return out

    def seeds_in(f):
        return (f[0], [1]) if len(f) == 1 else (f[1], [0])

    windows = {"x": [None, None], "mine": place((seeds, [0])), "other": place((seeds_other, [0]))}
    for m in range(half - 1):
        windows["x"].append(
            place(
                (first_far[m][0], [0]), (rest_far[m], range(groups - 1)),
                (near_first[m][0], [0]), (near_second[m], [0]),
            )
        )
        one, more = rest_far_other[m]
        windows["x"].append(
            place(
                (first_far_other[m], [0]), (one, [0]), (more, range(groups - 2)),
                (near_first_other[m][0], [0]), (near_second_other[m], [0]),
            )
        )
        windows["mine"] += place((seeds_far[m], [0]))
        windows["other"] += place((seeds_far_other[m], [0]))
    windows["mine"] += place(seeds_in(near_first[0]))
    windows["other"] += place(seeds_in(near_first_other[0]))

    def affinity_of(m, done):
        early = early_of(m, done) if m else first_early
        logits = logits_of(m, early) if m else first_logits
        return pl.pallas_call(
            functools.partial(affinity_kernel, groups, m, windows),
            out_shape=(jax.ShapeDtypeStruct((wtiles, TILE, TILE), jnp.bfloat16), labels_shape),
            in_specs=[vmem] * (2 + len(arrays)),
            out_specs=(vmem, vmem),
            scratch_shapes=[pltpu.VMEM((SPILL, TILE, TILE), jnp.float32)],
            compiler_params=params,
            cost_estimate=little,
            name=f"affinity_{m}",
        )(logits, early[1], *arrays)

    affinity, labels = [], []
    for m in range(half):
        a, l = affinity_of(m, labels[-1:])
        affinity.append(a)
        labels.append(l)
    near_labels = from_next(labels[0])
    near_labels_other = across(near_labels, 1)
    others = [across(l, 1) for l in labels]
    total = pl.pallas_call(
        functools.partial(own_kernel, groups),
        out_shape=jax.ShapeDtypeStruct((TILE, concepts), jnp.float32),
        in_specs=[vmem] * (1 + 3 * half),
        out_specs=vmem,
        compiler_params=params,
        cost_estimate=little,
        name="spread_own",
    )(seeds, *affinity, *labels, *others)
    for distance, block in enumerate((near_labels, near_labels_other)):
        total = pl.pallas_call(
            functools.partial(near_kernel, groups, distance),
            out_shape=jax.ShapeDtypeStruct((TILE, concepts), jnp.bfloat16 if distance else jnp.float32),
            in_specs=[vmem] * (2 + half),
            out_specs=vmem,
            compiler_params=params,
            cost_estimate=little,
            name=f"spread_near_{distance}",
        )(total, block, *affinity)
    return total


def solution(mesh):
    in_specs = (
        P("shard", "grp"),
        P("shard"),
        P("shard", None),
        P("shard"),
        P(("shard", "grp")),
        P(("shard", "grp"), None),
    )
    out_specs = P(("shard", "grp"), None)
    return jax.shard_map(local, mesh=mesh, in_specs=in_specs, out_specs=out_specs, check_vma=False)
```
